512 devices in a mesh: seq: 128 (over z, y, core), head: 4 (over x).
Axes of the slice: x: 4, y: 4, z: 16, core: 2. Of those that a mesh axis runs over, the one named last changes fastest.
Arguments:
- queries: bfloat16 [65536, 2048], P('seq', 'head'), may hold values from -6 to 6
- keys: bfloat16 [65536, 2048], P('seq', 'head'), may hold values from -6 to 6
- values: bfloat16 [65536, 2048], P('seq', 'head'), may hold values from -6 to 6
- out_grad: bfloat16 [65536, 2048], P('seq', 'head'), may hold values from -6 to 6
- labels: int32 [8, 65536, 1], P('head', 'seq'), may hold values from 0 to 511; in each aligned block of 512 rows (0 to 511, 512 to 1023, ..., all dimensions but the last counted through in order) at most 4 rows name the same one
Outputs:
- attended: bfloat16 [65536, 2048], P('seq', 'head')
- grad_queries: bfloat16 [65536, 2048], P('seq', 'head')
- grad_keys: bfloat16 [65536, 2048], P('seq', 'head')
- grad_values: bfloat16 [65536, 2048], P('seq', 'head')
The draws below stay inside these ranges and needn't reach their ends.
Inputs may be any that keep to these rules, and one draw needn't show every extreme that they name: `labels`: in each routed head the 512 tokens of one device name no cluster more than 4 times, and in some device some cluster is named exactly 4 times.
All inputs are finite; a program needn't handle non-finite values.
Results may differ from the reference program's by a relative error of at most 0.039.
Values may be sent and summed in bfloat16 or wider, within the bound.
No kernel may reach another device: no remote copies, remote signals or barrier semaphores. Data moves between devices by JAX's collectives and lax.ppermute only.
A program may use at most 128 MiB of HBM per device.

```python
import math
import jax
import jax.numpy as jnp
import numpy as np
from jax import lax

HD = 128
HEADS = 16
CLUSTERS = 512
WINDOW = 256
SLOTS = 4
TOK_DEV = 512
TOKENS = 65536
N_SEQ = 128


def draw_queries(key, part):
    key = jax.random.fold_in(key, 1)
    drawn = jnp.clip(jax.random.normal(key, (TOKENS, HEADS, HD), jnp.float32), -6.0, 6.0)
    return drawn.reshape(TOKENS, HEADS * HD).astype(jnp.bfloat16)


def draw_keys(key, part):
    key = jax.random.fold_in(key, 2)
    drawn = jnp.clip(jax.random.normal(key, (TOKENS, HEADS, HD), jnp.float32), -6.0, 6.0)
    return drawn.reshape(TOKENS, HEADS * HD).astype(jnp.bfloat16)


def block_levels(stream_key, dims, cuts, low, high):
    gain, own = 1.0, jax.random.fold_in(stream_key, 6)
    for dim, blocks in cuts:
        steps = jnp.exp(jax.random.uniform(jax.random.fold_in(own, dim), (blocks,), jnp.float32, low / len(cuts), high / len(cuts)))
        gain = gain * jnp.repeat(steps, dims[dim] // blocks).reshape([-1 if axis == dim else 1 for axis in range(len(dims))])
    return gain


def shared_out(rng, own, number, rows, count, top, bound, slope):
    sequence = jax.random.permutation(rng, count)
    crowded, ordinary = shares(count, rows * top, bound, slope, True), shares(count, rows * top, bound, slope, False)
    places = jnp.arange(count)

    def named(sizes, turn):
        used = int((sizes > 0).sum())
        fixed = max(1, used // 4)
        moved = fixed + (places - fixed + turn * (used - fixed)) % max(1, count - fixed)
        return jnp.zeros((count,), jnp.int32).at[sequence[jnp.where(places < fixed, places, moved)]].set(jnp.asarray(sizes, jnp.int32))

    sizes = jnp.where(number % 4 == 0, named(crowded, number // 4), named(ordinary, number - number // 4 - 1))
    mixed = jax.random.permutation(jax.random.fold_in(own, 3), count)
    source_of, taker = mixed[0:count // 2 * 2:2], mixed[1:count // 2 * 2:2]
    slack = jnp.minimum(sizes[source_of] - 1, bound - sizes[taker]) // 2
    slack = jnp.where((source_of == sequence[0]) | (taker == sequence[0]) | (sizes[taker] == 0), 0, jnp.maximum(slack, 0))
    moved = jax.random.randint(jax.random.fold_in(own, 4), (count // 2,), 0, 1 << 20) % (slack + 1)
    sizes = sizes.at[source_of].add(-moved).at[taker].add(moved)
    members = jnp.searchsorted(jnp.cumsum(sizes), jnp.arange(rows * top), side="right").astype(jnp.int32)
    grid = members.reshape(top, rows).T
    grid = grid[jax.random.permutation(jax.random.fold_in(own, 1), rows)]
    turn = jax.random.randint(jax.random.fold_in(own, 2), (rows, 1), 0, top)
    return jnp.take_along_axis(grid, (jnp.arange(top)[None, :] + turn) % top, axis=1)


def shares(count, total, limit, slope, full):
    weights = [(1 << 20) // math.isqrt(grade ** slope) + 1 for grade in range(1, count + 1)]
    largest = limit if full else min(limit, max(-(-total // count), total * weights[0] // sum(weights)))
    least = 1 if total - largest >= count - 1 else 0
    given, rest = [largest] + [least] * (count - 1), total - largest - least * (count - 1)
    while rest > 0:
        free = [i for i in range(1, count) if given[i] < largest] or [i for i in range(1, count) if given[i] < limit]
        mass, remaining = sum([weights[i] for i in free]), rest
        for i in free:
            extra = min(limit - given[i], max(1, remaining * weights[i] // mass), rest)
            given[i] = given[i] + extra
            rest = rest - extra
    return np.array(given)


def gaussian(own_key, shape, deviation, limit, shards=(), kind=jnp.bfloat16):
    level = block_levels(own_key, shape, shards, -0.22, 0.18) if shards else 1.0
    result = jax.random.normal(own_key, shape, jnp.float32) * deviation * level
    return jnp.minimum(jnp.maximum(result, -limit), limit).astype(kind)


def setup_inputs(seed: int = 0) -> dict:
    key_list = jax.random.split(jax.random.key(seed), 6)
    queries = draw_queries(jax.random.fold_in(key_list[5], 71), 0)
    keys = draw_keys(jax.random.fold_in(key_list[5], 71), 0)
    values = gaussian(key_list[2], (TOKENS, HEADS * HD), 1.0, 6.0, ((0, 128), (1, 4)))
    out_grad = gaussian(key_list[3], (TOKENS, HEADS * HD), 1.0, 6.0, ((0, 128), (1, 4)))
    labels_keys = jax.random.split(jax.random.fold_in(key_list[4], 1), (HEADS // 2) * TOKENS // TOK_DEV)
    labels_turns = jax.random.permutation(jax.random.fold_in(key_list[4], 3), (HEADS // 2) * TOKENS // TOK_DEV)
    labels = jax.vmap(lambda own, number: shared_out(jax.random.fold_in(key_list[4], 2), own, number, TOK_DEV, CLUSTERS, 1, SLOTS, 2))(labels_keys, labels_turns).reshape((HEADS // 2, TOKENS, 1))
    return dict(queries=queries, keys=keys, values=values, out_grad=out_grad, labels=labels)


MASKED = -1e+30

def forward_pass(queries_in, key_rows, value_rows, keep_mask):
    factor = 1.0 / math.sqrt(HD)
    scores = jnp.einsum('...rd,...cd->...rc', queries_in.astype(jnp.float32), key_rows.astype(jnp.float32)) * factor
    scores = jnp.where(keep_mask, scores, MASKED)
    row_max = lax.optimization_barrier(jnp.max(scores, axis=-1, keepdims=True))
    raised = jnp.exp(scores - row_max)
    weights = raised / lax.optimization_barrier(jnp.sum(raised, axis=-1, keepdims=True))
    rounded = lax.optimization_barrier(weights.astype(jnp.bfloat16))
    output = jnp.einsum('...rc,...cd->...rd', rounded.astype(jnp.float32), value_rows.astype(jnp.float32))
    output = lax.optimization_barrier(output.astype(jnp.bfloat16))
    return (weights, rounded, output)

def backward_pass(queries_in, key_rows, value_rows, grad_rows, weights, rounded, output):
    factor = 1.0 / math.sqrt(HD)
    row_dot = lax.optimization_barrier(jnp.sum(grad_rows.astype(jnp.float32) * output.astype(jnp.float32), axis=-1, keepdims=True))
    grad_weight = jnp.einsum('...rd,...cd->...rc', grad_rows.astype(jnp.float32), value_rows.astype(jnp.float32))
    grad_score = lax.optimization_barrier((weights * (grad_weight - row_dot) * factor).astype(jnp.bfloat16))
    score_wide = grad_score.astype(jnp.float32)
    grad_query = jnp.einsum('...rc,...cd->...rd', score_wide, key_rows.astype(jnp.float32))
    grad_key = jnp.einsum('...rc,...rd->...cd', score_wide, queries_in.astype(jnp.float32))
    grad_value = jnp.einsum('...rc,...rd->...cd', rounded.astype(jnp.float32), grad_rows.astype(jnp.float32))
    return (grad_query, grad_key, grad_value)

def window_mask(query_pos, key_pos):
    later = key_pos[None, :] <= query_pos[:, None]
    inside = key_pos[None, :] >= query_pos[:, None] - WINDOW
    return later & inside & (key_pos[None, :] >= 0)

def local_part(queries_in, key_rows, value_rows, grad_rows):
    head_count = queries_in.shape[0]
    padding = ((0, 0), (WINDOW, 0), (0, 0))
    keys_pad = jnp.pad(key_rows, padding)
    values_pad = jnp.pad(value_rows, padding)
    query_off = jnp.arange(TOK_DEV, dtype=jnp.int32)
    key_off = jnp.arange(TOK_DEV + WINDOW, dtype=jnp.int32) - WINDOW

    def advance(totals, block_ix):
        begin_row = block_ix * TOK_DEV
        query_blk = lax.dynamic_slice_in_dim(queries_in, begin_row, TOK_DEV, 1)
        grad_blk = lax.dynamic_slice_in_dim(grad_rows, begin_row, TOK_DEV, 1)
        key_blk = lax.dynamic_slice_in_dim(keys_pad, begin_row, TOK_DEV + WINDOW, 1)
        value_blk = lax.dynamic_slice_in_dim(values_pad, begin_row, TOK_DEV + WINDOW, 1)
        keep_mask = window_mask(begin_row + query_off, begin_row + key_off)[None]
        weights, rounded, output = forward_pass(query_blk, key_blk, value_blk, keep_mask)
        grad_query, grad_key, grad_value = backward_pass(query_blk, key_blk, value_blk, grad_blk, weights, rounded, output)
        key_tot, value_tot = totals
        key_tot = lax.dynamic_update_slice_in_dim(key_tot, lax.dynamic_slice_in_dim(key_tot, begin_row, TOK_DEV + WINDOW, 1) + grad_key, begin_row, 1)
        value_tot = lax.dynamic_update_slice_in_dim(value_tot, lax.dynamic_slice_in_dim(value_tot, begin_row, TOK_DEV + WINDOW, 1) + grad_value, begin_row, 1)
        return ((key_tot, value_tot), (output, grad_query.astype(jnp.bfloat16)))
    empty = jnp.zeros((head_count, TOKENS + WINDOW, HD), jnp.float32)
    totals, (outputs, grads_q) = lax.scan(advance, (empty, empty), jnp.arange(N_SEQ, dtype=jnp.int32))

    def unblock(blocked):
        return jnp.transpose(blocked, (1, 0, 2, 3)).reshape(head_count, TOKENS, HD)
    return (unblock(outputs), unblock(grads_q), totals[0][:, WINDOW:].astype(jnp.bfloat16), totals[1][:, WINDOW:].astype(jnp.bfloat16))

def serve_group(group):
    query_buf, key_buf, value_buf, grad_buf, token_pos = group
    block_rows = token_pos.shape[-1]
    keep_mask = (token_pos[:, None, :] >= 0) & (token_pos[:, None, :] <= token_pos[:, :, None]) | jnp.eye(block_rows, dtype=bool)[None]
    weights, rounded, output = forward_pass(query_buf, key_buf, value_buf, keep_mask)
    grad_query, grad_key, grad_value = backward_pass(query_buf, key_buf, value_buf, grad_buf, weights, rounded, output)
    return (output, grad_query.astype(jnp.bfloat16), grad_key.astype(jnp.bfloat16), grad_value.astype(jnp.bfloat16))

def routed_head(packed):
    queries_in, key_rows, value_rows, grad_rows, clusters = packed
    device_of = jnp.arange(TOKENS, dtype=jnp.int32) // TOK_DEV
    blocked = clusters.reshape(N_SEQ, TOK_DEV)
    position = jnp.arange(TOK_DEV, dtype=jnp.int32)
    earlier = position[None, :] < position[:, None]
    same = blocked[:, :, None] == blocked[:, None, :]
    slot_rank = lax.optimization_barrier(jnp.sum(same & earlier[None], axis=-1)).astype(jnp.int32).reshape(TOKENS)
    row_place = device_of * SLOTS + slot_rank
    block_rows = SLOTS * N_SEQ
    group_size = CLUSTERS // N_SEQ

    def place(rows):
        full = jnp.zeros((CLUSTERS, block_rows, HD), jnp.bfloat16).at[clusters, row_place].set(rows)
        return full.reshape(N_SEQ, group_size, block_rows, HD)
    token_pos = jnp.full((CLUSTERS, block_rows), -1, jnp.int32).at[clusters, row_place].set(jnp.arange(TOKENS, dtype=jnp.int32))
    token_pos = token_pos.reshape(N_SEQ, group_size, block_rows)
    served = lax.map(serve_group, (place(queries_in), place(key_rows), place(value_rows), place(grad_rows), token_pos))
    flat = [item.reshape(CLUSTERS, block_rows, HD) for item in served]
    return (flat[0][clusters, row_place], flat[1][clusters, row_place], flat[2][clusters, row_place], flat[3][clusters, row_place])

def reference(queries, keys, values, out_grad, labels):
    local_ids = np.array([head for head in range(HEADS) if head % 4 < 2])
    routed_ids = np.array([head for head in range(HEADS) if head % 4 >= 2])

    def heads_first(source, chosen):
        return jnp.transpose(source.reshape(TOKENS, HEADS, HD)[:, chosen], (1, 0, 2))
    local_res = local_part(heads_first(queries, local_ids), heads_first(keys, local_ids), heads_first(values, local_ids), heads_first(out_grad, local_ids))
    routed_res = lax.map(routed_head, (heads_first(queries, routed_ids), heads_first(keys, routed_ids), heads_first(values, routed_ids), heads_first(out_grad, routed_ids), labels[:, :, 0]))
    results = []
    for local_arr, routed_arr in zip(local_res, routed_res):
        whole = jnp.zeros((TOKENS, HEADS, HD), jnp.bfloat16)
        whole = whole.at[:, local_ids].set(jnp.transpose(local_arr, (1, 0, 2)))
        whole = whole.at[:, routed_ids].set(jnp.transpose(routed_arr, (1, 0, 2)))
        results.append(whole.reshape(TOKENS, HEADS * HD))
    return (results[0], results[1], results[2], results[3])
```

```python
import math

import jax
import jax.numpy as jnp
from jax import lax
from jax.experimental import pallas as pl
from jax.experimental.pallas import tpu as pltpu
from jax.sharding import PartitionSpec as P

HD = 128
CLUSTERS = 512
WINDOW = 256
TOK = 512
DEVS = 128
CAP = 12
NEAR = 8 * DEVS
WIDE = 6 * HD
GROUP = 384
GROUPS = 4
ROWS = GROUP * GROUPS
PARTS = 10
TRIES = 64
TURNS = ((37, 11), (59, 77), (83, 40), (101, 95), (29, 23), (71, 118))
BLOCK = 256
MASKED = -1e30
FACTOR = 1.0 / math.sqrt(HD)
BF = jnp.bfloat16
F32 = jnp.float32

NN = (((1,), (0,)), ((), ()))
NT = (((1,), (1,)), ((), ()))
TN = (((0,), (0,)), ((), ()))


def dot(a, b, dims=NN):
    return lax.dot_general(a, b, dims, preferred_element_type=F32)


def iota(shape, dim):
    return lax.broadcasted_iota(jnp.int32, shape, dim)


def ones_where(condition):
    return jnp.where(condition, 1.0, 0.0)


def shape(dims, kind=BF):
    return jax.ShapeDtypeStruct(dims, kind)


VMEM = pl.BlockSpec(memory_space=pltpu.VMEM)
SMEM = pl.BlockSpec(memory_space=pltpu.SMEM)
ANY = pl.BlockSpec(memory_space=pl.ANY)


def call(
    kernel, out_shape, in_specs, out_specs, scratch=(), flops=0, moved=0, aliases=None, grid=()
):
    return pl.pallas_call(
        kernel,
        grid=grid,
        out_shape=out_shape,
        in_specs=in_specs,
        out_specs=out_specs,
        scratch_shapes=list(scratch),
        input_output_aliases=aliases or {},
        compiler_params=pltpu.CompilerParams(vmem_limit_bytes=48 * 2**20),
        cost_estimate=pl.CostEstimate(flops=flops, bytes_accessed=moved, transcendentals=0),
    )


def low_half():
    return (iota((128, 2 * HD), 0) & 7) < 4


def fold(rows):
    first, second = rows[:, : 2 * HD], rows[:, 2 * HD :]
    low = low_half()
    even = jnp.where(low, first, pltpu.roll(second, 4, 0))
    odd = jnp.where(low, pltpu.roll(first, 124, 0), second)
    both = [part.reshape(16, 8, 2 * HD) for part in (even, odd)]
    return jnp.stack(both, axis=1).reshape(2 * 128, 2 * HD).astype(BF)


def unfold(rows):
    both = rows.astype(F32).reshape(16, 2, 8, 2 * HD)
    even = both[:, 0].reshape(128, 2 * HD)
    odd = both[:, 1].reshape(128, 2 * HD)
    low = low_half()
    first = jnp.where(low, even, pltpu.roll(odd, 4, 0))
    second = jnp.where(low, pltpu.roll(even, 124, 0), odd)
    return jnp.concatenate([first, second], axis=1).astype(BF)


def spread_out(buffer_ref, rows_ref):
    for i in range(GROUPS):
        near = slice(i * BLOCK, (i + 1) * BLOCK)
        rows_ref[i * GROUP : i * GROUP + BLOCK, :] = buffer_ref[near, : 4 * HD]
        rows_ref[i * GROUP + BLOCK : (i + 1) * GROUP, :] = unfold(buffer_ref[near, 4 * HD :])


def tail_kernel(k_ref, v_ref, tail_ref):
    half = 2 * HD
    tail_ref[:, :half] = k_ref[:, :half]
    tail_ref[:, half:] = v_ref[:, :half]


def count_kernel(labels_ref, counts_ref, within_ref):
    later = ones_where(iota((TOK, TOK), 0) < iota((TOK, TOK), 1)).astype(BF)
    rows = []
    within_ref[...] = jnp.zeros_like(within_ref)
    for h in range(2):
        hit = ones_where(labels_ref[h] == iota((CLUSTERS, TOK), 0))
        total = dot(jnp.ones((8, TOK), BF), hit.astype(BF), NT)
        rows += [total[0:1, k * 128 : (k + 1) * 128] for k in range(4)]
        before = dot(hit.astype(BF), later)
        within_ref[h : h + 1, :] = jnp.sum(hit * before, axis=0, keepdims=True)
    table = jnp.concatenate(rows, axis=0)
    counts_ref[...] = jnp.broadcast_to(table[None], (DEVS, 8, 128)).astype(BF)


def shifts_of(attempt):
    return [(attempt * a + b) & 127 for a, b in TURNS]


def dealt(ranked, attempt):
    shifts = shifts_of(attempt)
    lane = iota((DEVS, 128), 1)
    wide = jnp.where((attempt & 1) == 0, 24, 0)
    lists = []
    for h in range(2):
        lists.append(pltpu.roll(ranked[4 * h], 64, 1) if h else ranked[4 * h])
        lists += [pltpu.roll(ranked[4 * h + k], shifts[3 * h + k - 1], 1) for k in (1, 2)]
        final = pltpu.roll(ranked[4 * h + 3], shifts[3 * h + 2], 1)
        passed = (lane >= 64 * h) & (lane < 64 * h + wide)
        lists.append(jnp.where(passed, 0.0, final))
        lists.append(pltpu.roll(jnp.where(passed, final, 0.0), 32, 1))
    return lists


def place_kernel(
    where_ref, counts_ref, labels_ref, within_ref, q_ref, k_ref, v_ref, g_ref,
    send_ref, slot_ref, name_ref, over_ref, table, ranked, stage, sems,
):
    me = where_ref[0]
    mode = where_ref[1]
    table[...] = counts_ref[...].astype(F32).reshape(DEVS * 8, 128)
    per = [table[pl.ds(r, DEVS, stride=8), :] for r in range(8)]
    orders = []
    for h in range(2):
        key_row, key_col = [], []
        for k in range(4):
            block = per[4 * h + k]
            down = jnp.sum(block, axis=0, keepdims=True)
            across = jnp.sum(block.T, axis=1, keepdims=True)
            tie_row = (CLUSTERS - 1 - k * 128) - iota((1, 128), 1)
            tie_col = (CLUSTERS - 1 - k * 128) - iota((128, 1), 0)
            key_row.append(down * CLUSTERS + tie_row.astype(F32))
            key_col.append(across * CLUSTERS + tie_col.astype(F32))
        order = []
        for k in range(4):
            larger = jnp.zeros((128, 128), F32)
            for other in range(4):
                larger = larger + ones_where(key_col[other] > key_row[k])
            rank = jnp.sum(larger, axis=0, keepdims=True).astype(jnp.int32)
            order.append(ones_where(iota((CLUSTERS, 128), 0) == rank).astype(BF))
        amount = sum(dot(per[4 * h + k].astype(BF), order[k], NT) for k in range(4))
        for k in range(4):
            ranked[4 * h + k] = amount[:, k * 128 : (k + 1) * 128]
        orders.append(jnp.concatenate(order, axis=1))

    def unfit(state):
        attempt, most = state
        return jnp.logical_and(most > CAP, attempt < TRIES)

    def attempt_next(state):
        attempt, _ = state
        return attempt + 1, jnp.max(sum(dealt(ranked, attempt)))

    attempt, most = lax.while_loop(unfit, attempt_next, (jnp.int32(0), jnp.float32(CAP + 1)))
    attempt = attempt - 1
    over = most > CAP
    over_ref[...] = jnp.full((8, 128), jnp.where(over, 1.0, 0.0), F32)

    amounts = dealt(ranked, attempt)
    offsets = [jnp.zeros((DEVS, 128), F32)]
    for j in range(PARTS):
        offsets.append(offsets[-1] + amounts[j])
    begin = 3 * mode
    end = jnp.where(over, jnp.minimum(begin + 3, PARTS), jnp.where(mode == 0, PARTS, 0))
    start = offsets[0]
    for p in (1, 2, 3):
        start = jnp.where(mode == p, offsets[3 * p], start)
    own_row = iota((DEVS, 128), 0) == me
    own_lane = iota((DEVS, 128), 1) == me
    lane8 = iota((8, 128), 1)
    bases = []
    name = jnp.zeros((DEVS, 16), jnp.int32)
    slot_lane = iota((DEVS, 16), 1).astype(F32)
    for j in range(PARTS):
        base = jnp.sum(jnp.where(own_row, offsets[j] - start, 0.0), axis=0, keepdims=True)
        inside = jnp.logical_and(j >= begin, j < end)
        base = jnp.broadcast_to(base + jnp.where(inside, 0.0, -1e6), (8, 128))
        bases.append(base + (lane8 * 16).astype(F32))
        reach = jnp.sum(jnp.where(own_lane, offsets[j + 1] - start, 0.0), axis=1, keepdims=True)
        name = name + jnp.where(reach <= slot_lane, 1, 0)
    name_ref[...] = name

    shifts = shifts_of(attempt)
    wide = jnp.where((attempt & 1) == 0, 24, 0)
    spots = []
    slot_ref[...] = jnp.zeros_like(slot_ref)
    for h in range(2):
        mine = bases[5 * h : 5 * h + 5]
        passed = (lane8 >= 64 * h) & (lane8 < 64 * h + wide)
        final = jnp.where(passed, pltpu.roll(mine[4], 96, 1), mine[3])
        rolled = [pltpu.roll(mine[0], 64, 1) if h else mine[0]]
        for k, base in ((1, mine[1]), (2, mine[2]), (3, final)):
            rolled.append(pltpu.roll(base, (128 - shifts[3 * h + k - 1]) & 127, 1))
        column = jnp.concatenate(
            [jnp.broadcast_to(base[0:1], (128, 128)).T[:, 0:1] for base in rolled], axis=0
        )
        hit = ones_where(labels_ref[h] == iota((CLUSTERS, TOK), 0)).astype(BF)
        at = dot(orders[h], hit)
        flat = jnp.sum(at * column, axis=0, keepdims=True) + within_ref[h : h + 1, :]
        flat = flat.astype(jnp.int32)
        owner, slot = flat >> 4, flat & 15
        inner = owner & 31
        spot = jnp.where(slot < 8, inner * 8 + slot, BLOCK + inner * 4 + slot - 8)
        spot = jnp.where(flat >= 0, (owner >> 5) * GROUP + spot, -1)
        slot_ref[h : h + 1, :] = spot
        spots.append(spot)
    packed = [
        jnp.concatenate([ref[:, (2 + h) * HD : (3 + h) * HD] for ref in (q_ref, k_ref, v_ref, g_ref)], axis=1)
        for h in range(2)
    ]
    rows = iota((GROUP, TOK), 0)
    copies = []
    for i in range(GROUPS):
        total = 0.0
        for h in range(2):
            pick = ones_where(rows + i * GROUP == spots[h]).astype(BF)
            total = total + dot(pick, packed[h])
        copies.append(store_group(total, i, stage, send_ref, sems))
    for copy in copies:
        copy.wait()


def store_group(total, i, stage, to_ref, sems):
    near = pl.ds(i * BLOCK, BLOCK)
    stage[near, : 4 * HD] = total[:BLOCK].astype(BF)
    stage[near, 4 * HD :] = fold(total[BLOCK:])
    copy = pltpu.make_async_copy(stage.at[near], to_ref.at[near], sems.at[i])
    copy.start()
    return copy


def attend(q, k, v, g, keep):
    scores = jnp.where(keep, dot(q, k, NT) * FACTOR, MASKED)
    raised = jnp.exp(scores - jnp.max(scores, axis=1, keepdims=True))
    weights = raised * (1.0 / jnp.sum(raised, axis=1, keepdims=True))
    rounded = weights.astype(BF)
    out = dot(rounded, v).astype(BF)
    row_dot = jnp.sum(g.astype(F32) * out.astype(F32), axis=1, keepdims=True)
    grad_score = (weights * (dot(g, v, NT) - row_dot) * FACTOR).astype(BF)
    return out, dot(grad_score, k), dot(grad_score, q, TN), dot(rounded, g, TN)


def position(index):
    group = sum(jnp.where(index >= n * GROUP, 1, 0) for n in range(1, GROUPS))
    inner = index - group * GROUP
    rest = inner - BLOCK
    near = (inner >> 3) * 16 + (inner & 7)
    far = (rest >> 2) * 16 + 8 + (rest & 3)
    return group * 512 + jnp.where(inner < BLOCK, near, far)


def routed_kernel(
    got_ref, name_col_ref, name_row_ref, out_ref, rows, gk_sum, gv_sum, stage, sems
):
    spread_out(got_ref, rows)
    copies = []
    for i in reversed(range(GROUPS)):
        here = slice(i * GROUP, (i + 1) * GROUP)
        upto = slice(0, (i + 1) * GROUP)
        same = name_col_ref[here, :] == name_row_ref[:, upto]
        past = position(iota((1, (i + 1) * GROUP), 1)) <= position(iota((GROUP, 1), 0) + i * GROUP)
        out, gq, gk, gv = attend(
            rows[here, 0:HD],
            rows[upto, HD : 2 * HD],
            rows[upto, 2 * HD : 3 * HD],
            rows[here, 3 * HD :],
            same & past,
        )
        if i == GROUPS - 1:
            gk_sum[...] = gk
            gv_sum[...] = gv
        else:
            gk_sum[upto, :] += gk
            gv_sum[upto, :] += gv
        total = jnp.concatenate([out.astype(F32), gq, gk_sum[here, :], gv_sum[here, :]], axis=1)
        copies.append(store_group(total, i, stage, out_ref, sems))
    for copy in copies:
        copy.wait()


def window_kernel(
    where_ref, q_ref, k_ref, v_ref, g_ref, halo_ref, out_ref, gq_ref, gk_ref, gv_ref, edge_ref
):
    first = where_ref[0] == 0
    row = iota((BLOCK, 2 * BLOCK), 0)
    lane = iota((BLOCK, 2 * BLOCK), 1)
    band = (lane <= row + BLOCK) & (lane >= row)
    for h in range(2):
        at = slice(h * HD, (h + 1) * HD)
        at_v = slice((2 + h) * HD, (3 + h) * HD)
        k0 = jnp.concatenate([halo_ref[:, at], k_ref[0:BLOCK, at]], axis=0)
        v0 = jnp.concatenate([halo_ref[:, at_v], v_ref[0:BLOCK, at]], axis=0)
        keep = band & (lane >= jnp.where(first, BLOCK, 0))
        out, gq, gk, gv = attend(q_ref[0:BLOCK, at], k0, v0, g_ref[0:BLOCK, at], keep)
        out_ref[0:BLOCK, at] = out
        gq_ref[0:BLOCK, at] = gq.astype(BF)
        edge_ref[:, at] = gk[0:BLOCK].astype(BF)
        edge_ref[:, at_v] = gv[0:BLOCK].astype(BF)
        out, gq, gk1, gv1 = attend(
            q_ref[BLOCK:, at], k_ref[:, at], v_ref[:, at], g_ref[BLOCK:, at], band
        )
        out_ref[BLOCK:, at] = out
        gq_ref[BLOCK:, at] = gq.astype(BF)
        gk_ref[0:BLOCK, at] = gk[BLOCK:] + gk1[0:BLOCK]
        gk_ref[BLOCK:, at] = gk1[BLOCK:]
        gv_ref[0:BLOCK, at] = gv[BLOCK:] + gv1[0:BLOCK]
        gv_ref[BLOCK:, at] = gv1[BLOCK:]


def edge_kernel(gk_l, gv_l, edge_ref, gk_ref, gv_ref):
    half = 2 * HD
    for ref, mine, edge in (
        (gk_ref, gk_l, edge_ref[:, 0:half]),
        (gv_ref, gv_l, edge_ref[:, half:]),
    ):
        ref[0 : TOK - WINDOW, 0:half] = mine[0 : TOK - WINDOW, :].astype(BF)
        ref[TOK - WINDOW :, 0:half] = (mine[TOK - WINDOW :, :] + edge.astype(F32)).astype(BF)


def fetch(slot_ref, rows_ref, h, i):
    part = slice(i * BLOCK, (i + 1) * BLOCK)
    spot = slot_ref[h : h + 1, part].astype(F32)
    spot = jnp.broadcast_to(spot, (128, BLOCK)).T[:, 0:1].astype(jnp.int32)
    pick = ones_where(iota((BLOCK, ROWS), 1) == spot).astype(BF)
    return part, dot(pick, rows_ref[...])


def finish_kernel(slot_ref, back_ref, *refs):
    outs = refs[4:8]
    rows, stage, sems = refs[8:]
    spread_out(back_ref, rows)
    copies = []
    for i in range(TOK // BLOCK):
        for h in range(2):
            part, found = fetch(slot_ref, rows, h, i)
            for n in range(4):
                stage[n, part, h * HD : (h + 1) * HD] = found[:, n * HD : (n + 1) * HD].astype(BF)
        for n in range(4):
            copy = pltpu.make_async_copy(
                stage.at[n, pl.ds(i * BLOCK, BLOCK), :],
                outs[n].at[pl.ds(i * BLOCK, BLOCK), pl.ds(2 * HD, 2 * HD)],
                sems.at[n, i],
            )
            copy.start()
            copies.append(copy)
    for copy in copies:
        copy.wait()


def add_kernel(slot_ref, back_ref, *refs):
    before, after, rows = refs[0:4], refs[4:8], refs[8]
    spread_out(back_ref, rows)
    for h in range(2):
        to = slice((2 + h) * HD, (3 + h) * HD)
        for i in range(TOK // BLOCK):
            part, found = fetch(slot_ref, rows, h, i)
            for n in range(4):
                if h == 0:
                    after[n][part, 0 : 2 * HD] = before[n][part, 0 : 2 * HD]
                more = before[n][part, to].astype(F32) + found[:, n * HD : (n + 1) * HD]
                after[n][part, to] = more.astype(BF)


def across(rows):
    blocks = rows.reshape((DEVS, 8, WIDE))
    blocks = lax.all_to_all(blocks, "seq", split_axis=0, concat_axis=0, tiled=True)
    return blocks.reshape((NEAR, WIDE))


def local(queries, keys, values, out_grad, labels):
    half = 2 * HD
    full = shape((TOK, 4 * HD))
    me = lax.axis_index("seq").astype(jnp.int32)
    sources = (queries, keys, values, out_grad)
    labels = labels.reshape(2, 1, TOK)
    last_rows = pl.BlockSpec((WINDOW, 4 * HD), lambda i: (TOK // WINDOW - 1, 0))
    tail = call(
        tail_kernel,
        shape((WINDOW, 4 * HD)),
        [last_rows] * 2,
        pl.BlockSpec((WINDOW, 4 * HD), lambda i: (0, 0)),
        moved=2**19,
        grid=(1,),
    )(keys, values)
    steps = [(s, s + 1) for s in range(DEVS - 1)]
    halo = lax.ppermute(tail, "seq", steps)
    counts, within = call(
        count_kernel,
        (shape((DEVS, 8, 128)), shape((8, TOK), F32)),
        [VMEM],
        (VMEM,) * 2,
        flops=2 * 2 * TOK**3,
        moved=2**20,
    )(labels)
    counts, halo = lax.optimization_barrier((counts, halo))
    counts = lax.all_to_all(counts, "seq", split_axis=0, concat_axis=0, tiled=True)

    def window(halo):
        return call(
            window_kernel,
            (
                full,
                full,
                shape((TOK, half), F32),
                shape((TOK, half), F32),
                shape((WINDOW, 2 * half)),
            ),
            [SMEM] + [VMEM] * 5,
            (VMEM,) * 5,
            flops=4 * 6 * 2 * 256 * 512 * 128,
            moved=6 * 2**20,
        )(me.reshape(1), *sources, halo)

    def serve(mode, halo=None):
        send, slot, name, over = call(
            place_kernel,
            (
                shape((NEAR, WIDE)),
                shape((8, TOK), jnp.int32),
                shape((DEVS, 16), jnp.int32),
                shape((8, 128), F32),
            ),
            [SMEM] + [VMEM] * 7,
            (ANY, VMEM, VMEM, VMEM),
            scratch=(
                pltpu.VMEM((DEVS * 8, 128), F32),
                pltpu.VMEM((8, DEVS, 128), F32),
                pltpu.VMEM((NEAR, WIDE), BF),
                pltpu.SemaphoreType.DMA((GROUPS,)),
            ),
            flops=2 * 2 * ROWS * TOK * TOK,
            moved=6 * 2**20,
        )(jnp.stack([me, mode]), counts, labels, within, *sources)
        mine = None
        if halo is not None:
            send, halo = lax.optimization_barrier((send, halo))
        got = across(send)
        if halo is not None:
            *mine, edge = window(halo)
            got, edge = lax.optimization_barrier((got, edge))
            edge = lax.ppermute(edge, "seq", [(b, a) for a, b in steps])
        near = name[:, :8].reshape(GROUPS, BLOCK)
        far = name[:, 8:CAP].reshape(GROUPS, GROUP - BLOCK)
        names = jnp.concatenate([near, far], axis=1)
        results = call(
            routed_kernel,
            shape((NEAR, WIDE)),
            [VMEM] * 3,
            ANY,
            scratch=(
                pltpu.VMEM((ROWS, 4 * HD), BF),
                pltpu.VMEM((ROWS, HD), F32),
                pltpu.VMEM((ROWS, HD), F32),
                pltpu.VMEM((NEAR, WIDE), BF),
                pltpu.SemaphoreType.DMA((GROUPS,)),
            ),
            flops=6 * ROWS * ROWS * HD,
            moved=4 * 2**20,
        )(got, names.reshape(ROWS, 1), names.reshape(1, ROWS))
        if halo is not None:
            results, edge = lax.optimization_barrier((results, edge))
            mine.append(edge)
        return across(results), slot, over, mine

    back, slot, over, (out_l, gq_l, gk_l, gv_l, edge) = serve(jnp.int32(0), halo)
    for distance in (1, 2):
        turn = [(x, (x + distance) % 4) for x in range(4)]
        over = jnp.maximum(over, lax.ppermute(over, "head", turn))
    gk_l, gv_l = call(
        edge_kernel, (full, full), [VMEM] * 3, (VMEM,) * 2, flops=2**20, moved=2**21
    )(gk_l, gv_l, edge)
    rows_scratch = pltpu.VMEM((ROWS, 4 * HD), BF)
    results = call(
        finish_kernel,
        (full,) * 4,
        [VMEM, VMEM] + [ANY] * 4,
        (ANY,) * 4,
        scratch=(
            rows_scratch,
            pltpu.VMEM((4, TOK, half), BF),
            pltpu.SemaphoreType.DMA((4, TOK // BLOCK)),
        ),
        flops=2 * 2 * ROWS * TOK * TOK,
        moved=6 * 2**20,
        aliases={2: 0, 3: 1, 4: 2, 5: 3},
    )(slot, back, out_l, gq_l, gk_l, gv_l)
    last = jnp.where(over[0, 0] > 0.5, 4, 1).astype(jnp.int32)

    def again(mode, sums):
        more, spot, _, _ = serve(mode)
        return call(
            add_kernel, (full,) * 4, [VMEM] * 6, (VMEM,) * 4, scratch=(rows_scratch,)
        )(spot, more, *sums)

    return lax.fori_loop(1, last, again, results)


def solution(mesh):
    spec = P("seq", "head")
    return jax.shard_map(
        local,
        mesh=mesh,
        in_specs=(spec, spec, spec, spec, P("head", "seq", None)),
        out_specs=(spec, spec, spec, spec),
        check_vma=False,
    )
```

```python
import math

import jax
import jax.numpy as jnp
from jax import lax
from jax.experimental import pallas as pl
from jax.experimental.pallas import tpu as pltpu
from jax.sharding import PartitionSpec as P

HD = 128
CLUSTERS = 512
WINDOW = 256
TOK = 512
DEVS = 128
CAP = 12
NEAR = 8 * DEVS
WIDE = 6 * HD
GROUP = 384
GROUPS = 4
ROWS = GROUP * GROUPS
PARTS = 10
TRIES = 64
TURNS = ((37, 11), (59, 77), (83, 40), (101, 95), (29, 23), (71, 118))
BLOCK = 256
MASKED = -1e30
FACTOR = 1.0 / math.sqrt(HD)
BF = jnp.bfloat16
F32 = jnp.float32

NN = (((1,), (0,)), ((), ()))
NT = (((1,), (1,)), ((), ()))
TN = (((0,), (0,)), ((), ()))


def dot(a, b, dims=NN):
    return lax.dot_general(a, b, dims, preferred_element_type=F32)


def iota(shape, dim):
    return lax.broadcasted_iota(jnp.int32, shape, dim)


def ones_where(condition):
    return jnp.where(condition, 1.0, 0.0)


def shape(dims, kind=BF):
    return jax.ShapeDtypeStruct(dims, kind)


VMEM = pl.BlockSpec(memory_space=pltpu.VMEM)
SMEM = pl.BlockSpec(memory_space=pltpu.SMEM)
ANY = pl.BlockSpec(memory_space=pl.ANY)


def call(
    kernel, out_shape, in_specs, out_specs, scratch=(), flops=0, moved=0, aliases=None, grid=()
):
    return pl.pallas_call(
        kernel,
        grid=grid,
        out_shape=out_shape,
        in_specs=in_specs,
        out_specs=out_specs,
        scratch_shapes=list(scratch),
        input_output_aliases=aliases or {},
        compiler_params=pltpu.CompilerParams(vmem_limit_bytes=48 * 2**20),
        cost_estimate=pl.CostEstimate(flops=flops, bytes_accessed=moved, transcendentals=0),
    )


def low_half():
    return (iota((128, 2 * HD), 0) & 7) < 4


def fold(rows):
    first, second = rows[:, : 2 * HD], rows[:, 2 * HD :]
    low = low_half()
    even = jnp.where(low, first, pltpu.roll(second, 4, 0))
    odd = jnp.where(low, pltpu.roll(first, 124, 0), second)
    both = [part.reshape(16, 8, 2 * HD) for part in (even, odd)]
    return jnp.stack(both, axis=1).reshape(2 * 128, 2 * HD).astype(BF)


def unfold(rows):
    both = rows.astype(F32).reshape(16, 2, 8, 2 * HD)
    even = both[:, 0].reshape(128, 2 * HD)
    odd = both[:, 1].reshape(128, 2 * HD)
    low = low_half()
    first = jnp.where(low, even, pltpu.roll(odd, 4, 0))
    second = jnp.where(low, pltpu.roll(even, 124, 0), odd)
    return jnp.concatenate([first, second], axis=1).astype(BF)


def spread_out(buffer_ref, rows_ref):
    for i in range(GROUPS):
        near = slice(i * BLOCK, (i + 1) * BLOCK)
        rows_ref[i * GROUP : i * GROUP + BLOCK, :] = buffer_ref[near, : 4 * HD]
        rows_ref[i * GROUP + BLOCK : (i + 1) * GROUP, :] = unfold(buffer_ref[near, 4 * HD :])


def tail_kernel(k_ref, v_ref, tail_ref):
    half = 2 * HD
    tail_ref[:, :half] = k_ref[:, :half]
    tail_ref[:, half:] = v_ref[:, :half]


def count_kernel(labels_ref, counts_ref, within_ref):
    later = ones_where(iota((TOK, TOK), 0) < iota((TOK, TOK), 1)).astype(BF)
    rows = []
    within_ref[...] = jnp.zeros_like(within_ref)
    for h in range(2):
        hit = ones_where(labels_ref[h] == iota((CLUSTERS, TOK), 0))
        total = dot(jnp.ones((8, TOK), BF), hit.astype(BF), NT)
        rows += [total[0:1, k * 128 : (k + 1) * 128] for k in range(4)]
        before = dot(hit.astype(BF), later)
        within_ref[h : h + 1, :] = jnp.sum(hit * before, axis=0, keepdims=True)
    table = jnp.concatenate(rows, axis=0)
    counts_ref[...] = jnp.broadcast_to(table[None], (DEVS, 8, 128)).astype(BF)


def shifts_of(attempt):
    return [(attempt * a + b) & 127 for a, b in TURNS]


def dealt(ranked, attempt):
    shifts = shifts_of(attempt)
    lane = iota((DEVS, 128), 1)
    wide = jnp.where((attempt & 1) == 0, 24, 0)
    lists = []
    for h in range(2):
        lists.append(pltpu.roll(ranked[4 * h], 64, 1) if h else ranked[4 * h])
        lists += [pltpu.roll(ranked[4 * h + k], shifts[3 * h + k - 1], 1) for k in (1, 2)]
        final = pltpu.roll(ranked[4 * h + 3], shifts[3 * h + 2], 1)
        passed = (lane >= 64 * h) & (lane < 64 * h + wide)
        lists.append(jnp.where(passed, 0.0, final))
        lists.append(pltpu.roll(jnp.where(passed, final, 0.0), 32, 1))
    return lists


def place_kernel(
    where_ref, counts_ref, labels_ref, within_ref, q_ref, k_ref, v_ref, g_ref,
    send_ref, slot_ref, name_ref, over_ref, table, ranked, stage, sems,
):
    me = where_ref[0]
    mode = where_ref[1]
    table[...] = counts_ref[...].astype(F32).reshape(DEVS * 8, 128)
    per = [table[pl.ds(r, DEVS, stride=8), :] for r in range(8)]
    orders = []
    for h in range(2):
        key_row, key_col = [], []
        for k in range(4):
            block = per[4 * h + k]
            down = jnp.sum(block, axis=0, keepdims=True)
            across = jnp.sum(block.T, axis=1, keepdims=True)
            tie_row = (CLUSTERS - 1 - k * 128) - iota((1, 128), 1)
            tie_col = (CLUSTERS - 1 - k * 128) - iota((128, 1), 0)
            key_row.append(down * CLUSTERS + tie_row.astype(F32))
            key_col.append(across * CLUSTERS + tie_col.astype(F32))
        order = []
        for k in range(4):
            larger = jnp.zeros((128, 128), F32)
            for other in range(4):
                larger = larger + ones_where(key_col[other] > key_row[k])
            rank = jnp.sum(larger, axis=0, keepdims=True).astype(jnp.int32)
            order.append(ones_where(iota((CLUSTERS, 128), 0) == rank).astype(BF))
        amount = sum(dot(per[4 * h + k].astype(BF), order[k], NT) for k in range(4))
        for k in range(4):
            ranked[4 * h + k] = amount[:, k * 128 : (k + 1) * 128]
        orders.append(jnp.concatenate(order, axis=1))

    def unfit(state):
        attempt, most = state
        return jnp.logical_and(most > CAP, attempt < TRIES)

    def attempt_next(state):
        attempt, _ = state
        return attempt + 1, jnp.max(sum(dealt(ranked, attempt)))

    attempt, most = lax.while_loop(unfit, attempt_next, (jnp.int32(0), jnp.float32(CAP + 1)))
    attempt = attempt - 1
    over = most > CAP
    over_ref[...] = jnp.full((8, 128), jnp.where(over, 1.0, 0.0), F32)

    amounts = dealt(ranked, attempt)
    offsets = [jnp.zeros((DEVS, 128), F32)]
    for j in range(PARTS):
        offsets.append(offsets[-1] + amounts[j])
    begin = 3 * mode
    end = jnp.where(over, jnp.minimum(begin + 3, PARTS), jnp.where(mode == 0, PARTS, 0))
    start = offsets[0]
    for p in (1, 2, 3):
        start = jnp.where(mode == p, offsets[3 * p], start)
    own_row = iota((DEVS, 128), 0) == me
    own_lane = iota((DEVS, 128), 1) == me
    lane8 = iota((8, 128), 1)
    bases = []
    name = jnp.zeros((DEVS, 16), jnp.int32)
    slot_lane = iota((DEVS, 16), 1).astype(F32)
    for j in range(PARTS):
        base = jnp.sum(jnp.where(own_row, offsets[j] - start, 0.0), axis=0, keepdims=True)
        inside = jnp.logical_and(j >= begin, j < end)
        base = jnp.broadcast_to(base + jnp.where(inside, 0.0, -1e6), (8, 128))
        bases.append(base + (lane8 * 16).astype(F32))
        reach = jnp.sum(jnp.where(own_lane, offsets[j + 1] - start, 0.0), axis=1, keepdims=True)
        name = name + jnp.where(reach <= slot_lane, 1, 0)
    name_ref[...] = name

    shifts = shifts_of(attempt)
    wide = jnp.where((attempt & 1) == 0, 24, 0)
    spots = []
    slot_ref[...] = jnp.zeros_like(slot_ref)
    for h in range(2):
        mine = bases[5 * h : 5 * h + 5]
        passed = (lane8 >= 64 * h) & (lane8 < 64 * h + wide)
        final = jnp.where(passed, pltpu.roll(mine[4], 96, 1), mine[3])
        rolled = [pltpu.roll(mine[0], 64, 1) if h else mine[0]]
        for k, base in ((1, mine[1]), (2, mine[2]), (3, final)):
            rolled.append(pltpu.roll(base, (128 - shifts[3 * h + k - 1]) & 127, 1))
        column = jnp.concatenate(
            [jnp.broadcast_to(base[0:1], (128, 128)).T[:, 0:1] for base in rolled], axis=0
        )
        hit = ones_where(labels_ref[h] == iota((CLUSTERS, TOK), 0)).astype(BF)
        at = dot(orders[h], hit)
        flat = jnp.sum(at * column, axis=0, keepdims=True) + within_ref[h : h + 1, :]
        flat = flat.astype(jnp.int32)
        owner, slot = flat >> 4, flat & 15
        inner = owner & 31
        spot = jnp.where(slot < 8, inner * 8 + slot, BLOCK + inner * 4 + slot - 8)
        spot = jnp.where(flat >= 0, (owner >> 5) * GROUP + spot, -1)
        slot_ref[h : h + 1, :] = spot
        spots.append(spot)
    packed = [
        jnp.concatenate([ref[:, (2 + h) * HD : (3 + h) * HD] for ref in (q_ref, k_ref, v_ref, g_ref)], axis=1)
        for h in range(2)
    ]
    rows = iota((GROUP, TOK), 0)
    copies = []
    for i in range(GROUPS):
        total = 0.0
        for h in range(2):
            pick = ones_where(rows + i * GROUP == spots[h]).astype(BF)
            total = total + dot(pick, packed[h])
        copies.append(store_group(total, i, stage, send_ref, sems))
    for copy in copies:
        copy.wait()


def store_group(total, i, stage, to_ref, sems):
    near = pl.ds(i * BLOCK, BLOCK)
    stage[near, : 4 * HD] = total[:BLOCK].astype(BF)
    stage[near, 4 * HD :] = fold(total[BLOCK:])
    copy = pltpu.make_async_copy(stage.at[near], to_ref.at[near], sems.at[i])
    copy.start()
    return copy


def attend(q, k, v, g, keep):
    scores = jnp.where(keep, dot(q, k, NT) * FACTOR, MASKED)
    raised = jnp.exp(scores - jnp.max(scores, axis=1, keepdims=True))
    weights = raised * (1.0 / jnp.sum(raised, axis=1, keepdims=True))
    rounded = weights.astype(BF)
    out = dot(rounded, v).astype(BF)
    row_dot = jnp.sum(g.astype(F32) * out.astype(F32), axis=1, keepdims=True)
    grad_score = (weights * (dot(g, v, NT) - row_dot) * FACTOR).astype(BF)
    return out, dot(grad_score, k), dot(grad_score, q, TN), dot(rounded, g, TN)


def position(index):
    group = sum(jnp.where(index >= n * GROUP, 1, 0) for n in range(1, GROUPS))
    inner = index - group * GROUP
    rest = inner - BLOCK
    near = (inner >> 3) * 16 + (inner & 7)
    far = (rest >> 2) * 16 + 8 + (rest & 3)
    return group * 512 + jnp.where(inner < BLOCK, near, far)


def routed_kernel(
    got_ref, name_col_ref, name_row_ref, out_ref, rows, gk_sum, gv_sum, stage, sems
):
    spread_out(got_ref, rows)
    copies = []
    for i in reversed(range(GROUPS)):
        here = slice(i * GROUP, (i + 1) * GROUP)
        upto = slice(0, (i + 1) * GROUP)
        same = name_col_ref[here, :] == name_row_ref[:, upto]
        past = position(iota((1, (i + 1) * GROUP), 1)) <= position(iota((GROUP, 1), 0) + i * GROUP)
        out, gq, gk, gv = attend(
            rows[here, 0:HD],
            rows[upto, HD : 2 * HD],
            rows[upto, 2 * HD : 3 * HD],
            rows[here, 3 * HD :],
            same & past,
        )
        if i == GROUPS - 1:
            gk_sum[...] = gk
            gv_sum[...] = gv
        else:
            gk_sum[upto, :] += gk
            gv_sum[upto, :] += gv
        total = jnp.concatenate([out.astype(F32), gq, gk_sum[here, :], gv_sum[here, :]], axis=1)
        copies.append(store_group(total, i, stage, out_ref, sems))
    for copy in copies:
        copy.wait()


def window_kernel(
    where_ref, q_ref, k_ref, v_ref, g_ref, halo_ref, out_ref, gq_ref, gk_ref, gv_ref, edge_ref
):
    first = where_ref[0] == 0
    row = iota((BLOCK, 2 * BLOCK), 0)
    lane = iota((BLOCK, 2 * BLOCK), 1)
    band = (lane <= row + BLOCK) & (lane >= row)
    for h in range(2):
        at = slice(h * HD, (h + 1) * HD)
        at_v = slice((2 + h) * HD, (3 + h) * HD)
        k0 = jnp.concatenate([halo_ref[:, at], k_ref[0:BLOCK, at]], axis=0)
        v0 = jnp.concatenate([halo_ref[:, at_v], v_ref[0:BLOCK, at]], axis=0)
        keep = band & (lane >= jnp.where(first, BLOCK, 0))
        out, gq, gk, gv = attend(q_ref[0:BLOCK, at], k0, v0, g_ref[0:BLOCK, at], keep)
        out_ref[0:BLOCK, at] = out
        gq_ref[0:BLOCK, at] = gq.astype(BF)
        edge_ref[:, at] = gk[0:BLOCK].astype(BF)
        edge_ref[:, at_v] = gv[0:BLOCK].astype(BF)
        out, gq, gk1, gv1 = attend(
            q_ref[BLOCK:, at], k_ref[:, at], v_ref[:, at], g_ref[BLOCK:, at], band
        )
        out_ref[BLOCK:, at] = out
        gq_ref[BLOCK:, at] = gq.astype(BF)
        gk_ref[0:BLOCK, at] = gk[BLOCK:] + gk1[0:BLOCK]
        gk_ref[BLOCK:, at] = gk1[BLOCK:]
        gv_ref[0:BLOCK, at] = gv[BLOCK:] + gv1[0:BLOCK]
        gv_ref[BLOCK:, at] = gv1[BLOCK:]


def edge_kernel(gk_l, gv_l, edge_ref, gk_ref, gv_ref):
    half = 2 * HD
    for ref, mine, edge in (
        (gk_ref, gk_l, edge_ref[:, 0:half]),
        (gv_ref, gv_l, edge_ref[:, half:]),
    ):
        ref[0 : TOK - WINDOW, 0:half] = mine[0 : TOK - WINDOW, :].astype(BF)
        ref[TOK - WINDOW :, 0:half] = (mine[TOK - WINDOW :, :] + edge.astype(F32)).astype(BF)


def fetch(slot_ref, rows_ref, h, i):
    part = slice(i * BLOCK, (i + 1) * BLOCK)
    spot = slot_ref[h : h + 1, part].astype(F32)
    spot = jnp.broadcast_to(spot, (128, BLOCK)).T[:, 0:1].astype(jnp.int32)
    pick = ones_where(iota((BLOCK, ROWS), 1) == spot).astype(BF)
    return part, dot(pick, rows_ref[...])


def finish_kernel(slot_ref, back_ref, *refs):
    outs = refs[4:8]
    rows, stage, sems = refs[8:]
    spread_out(back_ref, rows)
    copies = []
    for i in range(TOK // BLOCK):
        for h in range(2):
            part, found = fetch(slot_ref, rows, h, i)
            for n in range(4):
                stage[n, part, h * HD : (h + 1) * HD] = found[:, n * HD : (n + 1) * HD].astype(BF)
        for n in range(4):
            copy = pltpu.make_async_copy(
                stage.at[n, pl.ds(i * BLOCK, BLOCK), :],
                outs[n].at[pl.ds(i * BLOCK, BLOCK), pl.ds(2 * HD, 2 * HD)],
                sems.at[n, i],
            )
            copy.start()
            copies.append(copy)
    for copy in copies:
        copy.wait()


def add_kernel(slot_ref, back_ref, *refs):
    before, after, rows = refs[0:4], refs[4:8], refs[8]
    spread_out(back_ref, rows)
    for h in range(2):
        to = slice((2 + h) * HD, (3 + h) * HD)
        for i in range(TOK // BLOCK):
            part, found = fetch(slot_ref, rows, h, i)
            for n in range(4):
                if h == 0:
                    after[n][part, 0 : 2 * HD] = before[n][part, 0 : 2 * HD]
                more = before[n][part, to].astype(F32) + found[:, n * HD : (n + 1) * HD]
                after[n][part, to] = more.astype(BF)


def across(rows):
    blocks = rows.reshape((DEVS, 8, WIDE))
    blocks = lax.all_to_all(blocks, "seq", split_axis=0, concat_axis=0, tiled=True)
    return blocks.reshape((NEAR, WIDE))


def local(queries, keys, values, out_grad, labels):
    half = 2 * HD
    full = shape((TOK, 4 * HD))
    me = lax.axis_index("seq").astype(jnp.int32)
    sources = (queries, keys, values, out_grad)
    labels = labels.reshape(2, 1, TOK)
    last_rows = pl.BlockSpec((WINDOW, 4 * HD), lambda i: (TOK // WINDOW - 1, 0))
    tail = call(
        tail_kernel,
        shape((WINDOW, 4 * HD)),
        [last_rows] * 2,
        pl.BlockSpec((WINDOW, 4 * HD), lambda i: (0, 0)),
        moved=2**19,
        grid=(1,),
    )(keys, values)
    steps = [(s, s + 1) for s in range(DEVS - 1)]
    halo = lax.ppermute(tail, "seq", steps)
    counts, within = call(
        count_kernel,
        (shape((DEVS, 8, 128)), shape((8, TOK), F32)),
        [VMEM],
        (VMEM,) * 2,
        flops=2 * 2 * TOK**3,
        moved=2**20,
    )(labels)
    counts = lax.all_to_all(counts, "seq", split_axis=0, concat_axis=0, tiled=True)
    counts, halo = lax.optimization_barrier((counts, halo))

    def window(halo):
        return call(
            window_kernel,
            (
                full,
                full,
                shape((TOK, half), F32),
                shape((TOK, half), F32),
                shape((WINDOW, 2 * half)),
            ),
            [SMEM] + [VMEM] * 5,
            (VMEM,) * 5,
            flops=4 * 6 * 2 * 256 * 512 * 128,
            moved=6 * 2**20,
        )(me.reshape(1), *sources, halo)

    def serve(mode, halo=None):
        send, slot, name, over = call(
            place_kernel,
            (
                shape((NEAR, WIDE)),
                shape((8, TOK), jnp.int32),
                shape((DEVS, 16), jnp.int32),
                shape((8, 128), F32),
            ),
            [SMEM] + [VMEM] * 7,
            (ANY, VMEM, VMEM, VMEM),
            scratch=(
                pltpu.VMEM((DEVS * 8, 128), F32),
                pltpu.VMEM((8, DEVS, 128), F32),
                pltpu.VMEM((NEAR, WIDE), BF),
                pltpu.SemaphoreType.DMA((GROUPS,)),
            ),
            flops=2 * 2 * ROWS * TOK * TOK,
            moved=6 * 2**20,
        )(jnp.stack([me, mode]), counts, labels, within, *sources)
        mine = None
        if halo is not None:
            send, halo = lax.optimization_barrier((send, halo))
        got = across(send)
        if halo is not None:
            *mine, edge = window(halo)
            edge = lax.ppermute(edge, "seq", [(b, a) for a, b in steps])
            got, edge = lax.optimization_barrier((got, edge))
        near = name[:, :8].reshape(GROUPS, BLOCK)
        far = name[:, 8:CAP].reshape(GROUPS, GROUP - BLOCK)
        names = jnp.concatenate([near, far], axis=1)
        results = call(
            routed_kernel,
            shape((NEAR, WIDE)),
            [VMEM] * 3,
            ANY,
            scratch=(
                pltpu.VMEM((ROWS, 4 * HD), BF),
                pltpu.VMEM((ROWS, HD), F32),
                pltpu.VMEM((ROWS, HD), F32),
                pltpu.VMEM((NEAR, WIDE), BF),
                pltpu.SemaphoreType.DMA((GROUPS,)),
            ),
            flops=6 * ROWS * ROWS * HD,
            moved=4 * 2**20,
        )(got, names.reshape(ROWS, 1), names.reshape(1, ROWS))
        if halo is not None:
            mine.append(edge)
        return across(results), slot, over, mine

    back, slot, over, (out_l, gq_l, gk_l, gv_l, edge) = serve(jnp.int32(0), halo)
    for distance in (1, 2):
        turn = [(x, (x + distance) % 4) for x in range(4)]
        over = jnp.maximum(over, lax.ppermute(over, "head", turn))
    gk_l, gv_l = call(
        edge_kernel, (full, full), [VMEM] * 3, (VMEM,) * 2, flops=2**20, moved=2**21
    )(gk_l, gv_l, edge)
    rows_scratch = pltpu.VMEM((ROWS, 4 * HD), BF)
    results = call(
        finish_kernel,
        (full,) * 4,
        [VMEM, VMEM] + [ANY] * 4,
        (ANY,) * 4,
        scratch=(
            rows_scratch,
            pltpu.VMEM((4, TOK, half), BF),
            pltpu.SemaphoreType.DMA((4, TOK // BLOCK)),
        ),
        flops=2 * 2 * ROWS * TOK * TOK,
        moved=6 * 2**20,
        aliases={2: 0, 3: 1, 4: 2, 5: 3},
    )(slot, back, out_l, gq_l, gk_l, gv_l)
    last = jnp.where(over[0, 0] > 0.5, 4, 1).astype(jnp.int32)

    def again(mode, sums):
        more, spot, _, _ = serve(mode)
        return call(
            add_kernel, (full,) * 4, [VMEM] * 6, (VMEM,) * 4, scratch=(rows_scratch,)
        )(spot, more, *sums)

    return lax.fori_loop(1, last, again, results)


def solution(mesh):
    spec = P("seq", "head")
    return jax.shard_map(
        local,
        mesh=mesh,
        in_specs=(spec, spec, spec, spec, P("head", "seq", None)),
        out_specs=(spec, spec, spec, spec),
        check_vma=False,
    )
```

```python
import math

import jax
import jax.numpy as jnp
from jax import lax
from jax.experimental import pallas as pl
from jax.experimental.pallas import tpu as pltpu
from jax.sharding import PartitionSpec as P

HD = 128
CLUSTERS = 512
WINDOW = 256
TOK = 512
DEVS = 128
CAP = 12
NEAR = 8 * DEVS
WIDE = 6 * HD
GROUP = 384
GROUPS = 4
ROWS = GROUP * GROUPS
PARTS = 10
TRIES = 64
GAP = 40
TURNS = ((37, 11), (59, 77), (83, 40), (101, 95), (29, 23), (71, 118))
BLOCK = 256
MASKED = -1e30
FACTOR = 1.0 / math.sqrt(HD)
BF = jnp.bfloat16
F32 = jnp.float32

NN = (((1,), (0,)), ((), ()))
NT = (((1,), (1,)), ((), ()))
TN = (((0,), (0,)), ((), ()))


def dot(a, b, dims=NN):
    return lax.dot_general(a, b, dims, preferred_element_type=F32)


def iota(shape, dim):
    return lax.broadcasted_iota(jnp.int32, shape, dim)


def ones_where(condition):
    return jnp.where(condition, 1.0, 0.0)


def shape(dims, kind=BF):
    return jax.ShapeDtypeStruct(dims, kind)


VMEM = pl.BlockSpec(memory_space=pltpu.VMEM)
SMEM = pl.BlockSpec(memory_space=pltpu.SMEM)
ANY = pl.BlockSpec(memory_space=pl.ANY)


def call(
    kernel, out_shape, in_specs, out_specs, scratch=(), flops=0, moved=0, aliases=None, grid=()
):
    return pl.pallas_call(
        kernel,
        grid=grid,
        out_shape=out_shape,
        in_specs=in_specs,
        out_specs=out_specs,
        scratch_shapes=list(scratch),
        input_output_aliases=aliases or {},
        compiler_params=pltpu.CompilerParams(vmem_limit_bytes=48 * 2**20),
        cost_estimate=pl.CostEstimate(flops=flops, bytes_accessed=moved, transcendentals=0),
    )


def low_half():
    return (iota((128, 2 * HD), 0) & 7) < 4


def fold(rows):
    first, second = rows[:, : 2 * HD], rows[:, 2 * HD :]
    low = low_half()
    even = jnp.where(low, first, pltpu.roll(second, 4, 0))
    odd = jnp.where(low, pltpu.roll(first, 124, 0), second)
    both = [part.reshape(16, 8, 2 * HD) for part in (even, odd)]
    return jnp.stack(both, axis=1).reshape(2 * 128, 2 * HD).astype(BF)


def unfold(rows):
    both = rows.astype(F32).reshape(16, 2, 8, 2 * HD)
    even = both[:, 0].reshape(128, 2 * HD)
    odd = both[:, 1].reshape(128, 2 * HD)
    low = low_half()
    first = jnp.where(low, even, pltpu.roll(odd, 4, 0))
    second = jnp.where(low, pltpu.roll(even, 124, 0), odd)
    return jnp.concatenate([first, second], axis=1).astype(BF)


def spread_out(buffer_ref, rows_ref):
    for i in range(GROUPS):
        near = slice(i * BLOCK, (i + 1) * BLOCK)
        rows_ref[i * GROUP : i * GROUP + BLOCK, :] = buffer_ref[near, : 4 * HD]
        rows_ref[i * GROUP + BLOCK : (i + 1) * GROUP, :] = unfold(buffer_ref[near, 4 * HD :])


def tail_kernel(k_ref, v_ref, tail_ref):
    half = 2 * HD
    tail_ref[:, :half] = k_ref[:, :half]
    tail_ref[:, half:] = v_ref[:, :half]


def hits(labels_ref, h):
    return ones_where(labels_ref[h] == iota((CLUSTERS, TOK), 0)).astype(BF)


def count_kernel(labels_ref, counts_ref):
    rows = []
    for h in range(2):
        total = dot(jnp.ones((8, TOK), BF), hits(labels_ref, h), NT)
        rows += [total[0:1, k * 128 : (k + 1) * 128] for k in range(4)]
    table = jnp.concatenate(rows, axis=0)
    counts_ref[...] = jnp.broadcast_to(table[None], (DEVS, 8, 128)).astype(BF)


def rank_kernel(labels_ref, within_ref):
    later = ones_where(iota((TOK, TOK), 0) < iota((TOK, TOK), 1)).astype(BF)
    within_ref[...] = jnp.zeros_like(within_ref)
    for h in range(2):
        hit = hits(labels_ref, h)
        before = dot(hit, later) * hit.astype(F32)
        within_ref[h : h + 1, :] = jnp.sum(before, axis=0, keepdims=True)


def shifts_of(attempt):
    return [(attempt * a + b) & 127 for a, b in TURNS]


def dealt(ranked, attempt):
    shifts = shifts_of(attempt)
    lane = iota((DEVS, 128), 1)
    wide = jnp.where((attempt & 1) == 0, 24, 0)
    lists = []
    for h in range(2):
        lists.append(pltpu.roll(ranked[4 * h], 64, 1) if h else ranked[4 * h])
        lists += [pltpu.roll(ranked[4 * h + k], shifts[3 * h + k - 1], 1) for k in (1, 2)]
        final = pltpu.roll(ranked[4 * h + 3], shifts[3 * h + 2], 1)
        passed = (lane >= 64 * h) & (lane < 64 * h + wide)
        lists.append(jnp.where(passed, 0.0, final))
        lists.append(pltpu.roll(jnp.where(passed, final, 0.0), GAP, 1))
    return lists


def place_kernel(
    where_ref, counts_ref, labels_ref, within_ref, q_ref, k_ref, v_ref, g_ref,
    send_ref, slot_ref, name_ref, over_ref, table, ranked, stage, sems,
):
    me = where_ref[0]
    mode = where_ref[1]
    table[...] = counts_ref[...].astype(F32).reshape(DEVS * 8, 128)
    per = [table[pl.ds(r, DEVS, stride=8), :] for r in range(8)]
    orders = []
    for h in range(2):
        key_row, key_col = [], []
        for k in range(4):
            block = per[4 * h + k]
            down = jnp.sum(block, axis=0, keepdims=True)
            across = jnp.sum(block.T, axis=1, keepdims=True)
            tie_row = (CLUSTERS - 1 - k * 128) - iota((1, 128), 1)
            tie_col = (CLUSTERS - 1 - k * 128) - iota((128, 1), 0)
            key_row.append(down * CLUSTERS + tie_row.astype(F32))
            key_col.append(across * CLUSTERS + tie_col.astype(F32))
        order = []
        for k in range(4):
            larger = jnp.zeros((128, 128), F32)
            for other in range(4):
                larger = larger + ones_where(key_col[other] > key_row[k])
            rank = jnp.sum(larger, axis=0, keepdims=True).astype(jnp.int32)
            order.append(ones_where(iota((CLUSTERS, 128), 0) == rank).astype(BF))
        amount = sum(dot(per[4 * h + k].astype(BF), order[k], NT) for k in range(4))
        for k in range(4):
            ranked[4 * h + k] = amount[:, k * 128 : (k + 1) * 128]
        orders.append(jnp.concatenate(order, axis=1))

    def unfit(state):
        attempt, most = state
        return jnp.logical_and(most > CAP, attempt < TRIES)

    def attempt_next(state):
        attempt, _ = state
        return attempt + 1, jnp.max(sum(dealt(ranked, attempt)))

    attempt, most = lax.while_loop(unfit, attempt_next, (jnp.int32(0), jnp.float32(CAP + 1)))
    attempt = attempt - 1
    over = most > CAP
    over_ref[...] = jnp.full((8, 128), jnp.where(over, 1.0, 0.0), F32)

    amounts = dealt(ranked, attempt)
    offsets = [jnp.zeros((DEVS, 128), F32)]
    for j in range(PARTS):
        offsets.append(offsets[-1] + amounts[j])
    begin = 3 * mode
    end = jnp.where(over, jnp.minimum(begin + 3, PARTS), jnp.where(mode == 0, PARTS, 0))
    start = offsets[0]
    for p in (1, 2, 3):
        start = jnp.where(mode == p, offsets[3 * p], start)
    own_row = iota((DEVS, 128), 0) == me
    own_lane = iota((DEVS, 128), 1) == me
    lane8 = iota((8, 128), 1)
    bases = []
    name = jnp.zeros((DEVS, 16), jnp.int32)
    slot_lane = iota((DEVS, 16), 1).astype(F32)
    for j in range(PARTS):
        base = jnp.sum(jnp.where(own_row, offsets[j] - start, 0.0), axis=0, keepdims=True)
        inside = jnp.logical_and(j >= begin, j < end)
        base = jnp.broadcast_to(base + jnp.where(inside, 0.0, -1e6), (8, 128))
        bases.append(base + (lane8 * 16).astype(F32))
        reach = jnp.sum(jnp.where(own_lane, offsets[j + 1] - start, 0.0), axis=1, keepdims=True)
        name = name + jnp.where(reach <= slot_lane, 1, 0)
    name_ref[...] = name

    shifts = shifts_of(attempt)
    wide = jnp.where((attempt & 1) == 0, 24, 0)
    spots = []
    slot_ref[...] = jnp.zeros_like(slot_ref)
    for h in range(2):
        mine = bases[5 * h : 5 * h + 5]
        passed = (lane8 >= 64 * h) & (lane8 < 64 * h + wide)
        final = jnp.where(passed, pltpu.roll(mine[4], 128 - GAP, 1), mine[3])
        rolled = [pltpu.roll(mine[0], 64, 1) if h else mine[0]]
        for k, base in ((1, mine[1]), (2, mine[2]), (3, final)):
            rolled.append(pltpu.roll(base, (128 - shifts[3 * h + k - 1]) & 127, 1))
        column = jnp.concatenate(
            [jnp.broadcast_to(base[0:1], (128, 128)).T[:, 0:1] for base in rolled], axis=0
        )
        hit = ones_where(labels_ref[h] == iota((CLUSTERS, TOK), 0)).astype(BF)
        at = dot(orders[h], hit)
        flat = jnp.sum(at * column, axis=0, keepdims=True) + within_ref[h : h + 1, :]
        flat = flat.astype(jnp.int32)
        owner, slot = flat >> 4, flat & 15
        inner = owner & 31
        spot = jnp.where(slot < 8, inner * 8 + slot, BLOCK + inner * 4 + slot - 8)
        spot = jnp.where(flat >= 0, (owner >> 5) * GROUP + spot, -1)
        slot_ref[h : h + 1, :] = spot
        spots.append(spot)
    packed = [
        jnp.concatenate([ref[:, (2 + h) * HD : (3 + h) * HD] for ref in (q_ref, k_ref, v_ref, g_ref)], axis=1)
        for h in range(2)
    ]
    rows = iota((GROUP, TOK), 0)
    copies = []
    for i in range(GROUPS):
        total = 0.0
        for h in range(2):
            pick = ones_where(rows + i * GROUP == spots[h]).astype(BF)
            total = total + dot(pick, packed[h])
        copies.append(store_group(total, i, stage, send_ref, sems))
    for copy in copies:
        copy.wait()


def store_group(total, i, stage, to_ref, sems):
    near = pl.ds(i * BLOCK, BLOCK)
    stage[near, : 4 * HD] = total[:BLOCK].astype(BF)
    stage[near, 4 * HD :] = fold(total[BLOCK:])
    copy = pltpu.make_async_copy(stage.at[near], to_ref.at[near], sems.at[i])
    copy.start()
    return copy


def attend(q, k, v, g, keep):
    scores = jnp.where(keep, dot(q, k, NT) * (FACTOR * math.log2(math.e)), MASKED)
    raised = jnp.exp2(scores - jnp.max(scores, axis=1, keepdims=True))
    weights = raised * (1.0 / jnp.sum(raised, axis=1, keepdims=True))
    rounded = weights.astype(BF)
    out = dot(rounded, v).astype(BF)
    row_dot = jnp.sum(g.astype(F32) * out.astype(F32), axis=1, keepdims=True)
    grad_score = (weights * (dot(g, v, NT) - row_dot)).astype(BF)
    grad_k = dot(q, grad_score, TN).T * FACTOR
    return out, dot(grad_score, k) * FACTOR, grad_k, dot(g, rounded, TN).T


def position(index):
    rest = index - BLOCK
    near = (index >> 3) * 16 + (index & 7)
    far = (rest >> 2) * 16 + 8 + (rest & 3)
    return jnp.where(index < BLOCK, near, far)


def routed_kernel(
    got_ref, name_col_ref, name_row_ref, out_ref, rows, gk_sum, gv_sum, stage, sems
):
    spread_out(got_ref, rows)
    copies = []
    for i in reversed(range(GROUPS)):
        here = slice(i * GROUP, (i + 1) * GROUP)
        upto = slice(0, (i + 1) * GROUP)
        same = name_col_ref[here, :] == name_row_ref[:, upto]
        past = position(iota((1, GROUP), 1)) <= position(iota((GROUP, 1), 0))
        if i:
            past = jnp.concatenate([jnp.full((GROUP, i * GROUP), True), past], axis=1)
        out, gq, gk, gv = attend(
            rows[here, 0:HD],
            rows[upto, HD : 2 * HD],
            rows[upto, 2 * HD : 3 * HD],
            rows[here, 3 * HD :],
            same & past,
        )
        if i == GROUPS - 1:
            gk_sum[...] = gk
            gv_sum[...] = gv
        else:
            gk_sum[upto, :] += gk
            gv_sum[upto, :] += gv
        total = jnp.concatenate([out.astype(F32), gq, gk_sum[here, :], gv_sum[here, :]], axis=1)
        copies.append(store_group(total, i, stage, out_ref, sems))
    for copy in copies:
        copy.wait()


def window_kernel(
    where_ref, q_ref, k_ref, v_ref, g_ref, halo_ref, out_ref, gq_ref, gk_ref, gv_ref, edge_ref
):
    first = where_ref[0] == 0
    row = iota((BLOCK, 2 * BLOCK), 0)
    lane = iota((BLOCK, 2 * BLOCK), 1)
    band = (lane <= row + BLOCK) & (lane >= row)
    for h in range(2):
        at = slice(h * HD, (h + 1) * HD)
        at_v = slice((2 + h) * HD, (3 + h) * HD)
        k0 = jnp.concatenate([halo_ref[:, at], k_ref[0:BLOCK, at]], axis=0)
        v0 = jnp.concatenate([halo_ref[:, at_v], v_ref[0:BLOCK, at]], axis=0)
        keep = band & (lane >= jnp.where(first, BLOCK, 0))
        out, gq, gk, gv = attend(q_ref[0:BLOCK, at], k0, v0, g_ref[0:BLOCK, at], keep)
        out_ref[0:BLOCK, at] = out
        gq_ref[0:BLOCK, at] = gq.astype(BF)
        edge_ref[:, at] = gk[0:BLOCK].astype(BF)
        edge_ref[:, at_v] = gv[0:BLOCK].astype(BF)
        out, gq, gk1, gv1 = attend(
            q_ref[BLOCK:, at], k_ref[:, at], v_ref[:, at], g_ref[BLOCK:, at], band
        )
        out_ref[BLOCK:, at] = out
        gq_ref[BLOCK:, at] = gq.astype(BF)
        gk_ref[0:BLOCK, at] = gk[BLOCK:] + gk1[0:BLOCK]
        gk_ref[BLOCK:, at] = gk1[BLOCK:]
        gv_ref[0:BLOCK, at] = gv[BLOCK:] + gv1[0:BLOCK]
        gv_ref[BLOCK:, at] = gv1[BLOCK:]


def edge_kernel(gk_l, gv_l, edge_ref, gk_ref, gv_ref):
    half = 2 * HD
    for ref, mine, edge in (
        (gk_ref, gk_l, edge_ref[:, 0:half]),
        (gv_ref, gv_l, edge_ref[:, half:]),
    ):
        ref[0 : TOK - WINDOW, 0:half] = mine[0 : TOK - WINDOW, :].astype(BF)
        ref[TOK - WINDOW :, 0:half] = (mine[TOK - WINDOW :, :] + edge.astype(F32)).astype(BF)


def fetch(slot_ref, rows_ref, h, i):
    part = slice(i * BLOCK, (i + 1) * BLOCK)
    spot = slot_ref[h : h + 1, part].astype(F32)
    spot = jnp.broadcast_to(spot, (128, BLOCK)).T[:, 0:1].astype(jnp.int32)
    pick = ones_where(iota((BLOCK, ROWS), 1) == spot).astype(BF)
    return part, dot(pick, rows_ref[...])


def finish_kernel(slot_ref, back_ref, *refs):
    outs = refs[4:8]
    rows, stage, sems = refs[8:]
    spread_out(back_ref, rows)
    copies = []
    for i in range(TOK // BLOCK):
        for h in range(2):
            part, found = fetch(slot_ref, rows, h, i)
            for n in range(4):
                stage[n, part, h * HD : (h + 1) * HD] = found[:, n * HD : (n + 1) * HD].astype(BF)
        for n in range(4):
            copy = pltpu.make_async_copy(
                stage.at[n, pl.ds(i * BLOCK, BLOCK), :],
                outs[n].at[pl.ds(i * BLOCK, BLOCK), pl.ds(2 * HD, 2 * HD)],
                sems.at[n, i],
            )
            copy.start()
            copies.append(copy)
    for copy in copies:
        copy.wait()


def add_kernel(slot_ref, back_ref, *refs):
    before, after, rows = refs[0:4], refs[4:8], refs[8]
    spread_out(back_ref, rows)
    for h in range(2):
        to = slice((2 + h) * HD, (3 + h) * HD)
        for i in range(TOK // BLOCK):
            part, found = fetch(slot_ref, rows, h, i)
            for n in range(4):
                if h == 0:
                    after[n][part, 0 : 2 * HD] = before[n][part, 0 : 2 * HD]
                more = before[n][part, to].astype(F32) + found[:, n * HD : (n + 1) * HD]
                after[n][part, to] = more.astype(BF)


def across(rows):
    blocks = rows.reshape((DEVS, 8, WIDE))
    blocks = lax.all_to_all(blocks, "seq", split_axis=0, concat_axis=0, tiled=True)
    return blocks.reshape((NEAR, WIDE))


def local(queries, keys, values, out_grad, labels):
    half = 2 * HD
    full = shape((TOK, 4 * HD))
    me = lax.axis_index("seq").astype(jnp.int32)
    sources = (queries, keys, values, out_grad)
    labels = labels.reshape(2, 1, TOK)
    last_rows = pl.BlockSpec((WINDOW, 4 * HD), lambda i: (TOK // WINDOW - 1, 0))
    tail = call(
        tail_kernel,
        shape((WINDOW, 4 * HD)),
        [last_rows] * 2,
        pl.BlockSpec((WINDOW, 4 * HD), lambda i: (0, 0)),
        moved=2**19,
        grid=(1,),
    )(keys, values)
    steps = [(s, s + 1) for s in range(DEVS - 1)]
    halo = lax.ppermute(tail, "seq", steps)
    counts = call(
        count_kernel,
        shape((DEVS, 8, 128)),
        [VMEM],
        VMEM,
        flops=2 * 2 * 8 * TOK**2,
        moved=2**18,
    )(labels)
    counts = lax.all_to_all(counts, "seq", split_axis=0, concat_axis=0, tiled=True)
    within = call(
        rank_kernel, shape((8, TOK), F32), [VMEM], VMEM, flops=2 * 2 * TOK**3, moved=2**15
    )(labels)
    counts, halo, within = lax.optimization_barrier((counts, halo, within))

    def window(halo):
        return call(
            window_kernel,
            (
                full,
                full,
                shape((TOK, half), F32),
                shape((TOK, half), F32),
                shape((WINDOW, 2 * half)),
            ),
            [SMEM] + [VMEM] * 5,
            (VMEM,) * 5,
            flops=4 * 6 * 2 * 256 * 512 * 128,
            moved=6 * 2**20,
        )(me.reshape(1), *sources, halo)

    def serve(mode, halo=None):
        send, slot, name, over = call(
            place_kernel,
            (
                shape((NEAR, WIDE)),
                shape((8, TOK), jnp.int32),
                shape((DEVS, 16), jnp.int32),
                shape((8, 128), F32),
            ),
            [SMEM] + [VMEM] * 7,
            (ANY, VMEM, VMEM, VMEM),
            scratch=(
                pltpu.VMEM((DEVS * 8, 128), F32),
                pltpu.VMEM((8, DEVS, 128), F32),
                pltpu.VMEM((NEAR, WIDE), BF),
                pltpu.SemaphoreType.DMA((GROUPS,)),
            ),
            flops=2 * 2 * ROWS * TOK * TOK,
            moved=6 * 2**20,
        )(jnp.stack([me, mode]), counts, labels, within, *sources)
        mine = None
        if halo is not None:
            send, halo = lax.optimization_barrier((send, halo))
        got = across(send)
        if halo is not None:
            *mine, edge = window(halo)
            edge = lax.ppermute(edge, "seq", [(b, a) for a, b in steps])
            got, edge = lax.optimization_barrier((got, edge))
        near = name[:, :8].reshape(GROUPS, BLOCK)
        far = name[:, 8:CAP].reshape(GROUPS, GROUP - BLOCK)
        names = jnp.concatenate([near, far], axis=1)
        results = call(
            routed_kernel,
            shape((NEAR, WIDE)),
            [VMEM] * 3,
            ANY,
            scratch=(
                pltpu.VMEM((ROWS, 4 * HD), BF),
                pltpu.VMEM((ROWS, HD), F32),
                pltpu.VMEM((ROWS, HD), F32),
                pltpu.VMEM((NEAR, WIDE), BF),
                pltpu.SemaphoreType.DMA((GROUPS,)),
            ),
            flops=6 * ROWS * ROWS * HD,
            moved=4 * 2**20,
        )(got, names.reshape(ROWS, 1), names.reshape(1, ROWS))
        if halo is not None:
            mine.append(edge)
        return across(results), slot, over, mine

    back, slot, over, (out_l, gq_l, gk_l, gv_l, edge) = serve(jnp.int32(0), halo)
    for distance in (1, 2):
        turn = [(x, (x + distance) % 4) for x in range(4)]
        over = jnp.maximum(over, lax.ppermute(over, "head", turn))
    gk_l, gv_l = call(
        edge_kernel, (full, full), [VMEM] * 3, (VMEM,) * 2, flops=2**20, moved=2**21
    )(gk_l, gv_l, edge)
    rows_scratch = pltpu.VMEM((ROWS, 4 * HD), BF)
    results = call(
        finish_kernel,
        (full,) * 4,
        [VMEM, VMEM] + [ANY] * 4,
        (ANY,) * 4,
        scratch=(
            rows_scratch,
            pltpu.VMEM((4, TOK, half), BF),
            pltpu.SemaphoreType.DMA((4, TOK // BLOCK)),
        ),
        flops=2 * 2 * ROWS * TOK * TOK,
        moved=6 * 2**20,
        aliases={2: 0, 3: 1, 4: 2, 5: 3},
    )(slot, back, out_l, gq_l, gk_l, gv_l)
    last = jnp.where(over[0, 0] > 0.5, 4, 1).astype(jnp.int32)

    def again(mode, sums):
        more, spot, _, _ = serve(mode)
        return call(
            add_kernel, (full,) * 4, [VMEM] * 6, (VMEM,) * 4, scratch=(rows_scratch,)
        )(spot, more, *sums)

    return lax.fori_loop(1, last, again, results)


def solution(mesh):
    spec = P("seq", "head")
    return jax.shard_map(
        local,
        mesh=mesh,
        in_specs=(spec, spec, spec, spec, P("head", "seq", None)),
        out_specs=(spec, spec, spec, spec),
        check_vma=False,
    )
```

```python
import math

import jax
import jax.numpy as jnp
from jax import lax
from jax.experimental import pallas as pl
from jax.experimental.pallas import tpu as pltpu
from jax.sharding import PartitionSpec as P

HD = 128
CLUSTERS = 512
WINDOW = 256
TOK = 512
DEVS = 128
CAP = 12
NEAR = 8 * DEVS
WIDE = 6 * HD
GROUP = 384
GROUPS = 4
ROWS = GROUP * GROUPS
PARTS = 10
TRIES = 64
GAP = 40
TURNS = ((37, 11), (59, 77), (83, 40), (101, 95), (29, 23), (71, 118))
BLOCK = 256
MASKED = -1e30
FACTOR = 1.0 / math.sqrt(HD)
BF = jnp.bfloat16
F32 = jnp.float32

NN = (((1,), (0,)), ((), ()))
NT = (((1,), (1,)), ((), ()))
TN = (((0,), (0,)), ((), ()))


def dot(a, b, dims=NN):
    return lax.dot_general(a, b, dims, preferred_element_type=F32)


def iota(shape, dim):
    return lax.broadcasted_iota(jnp.int32, shape, dim)


def ones_where(condition):
    return jnp.where(condition, 1.0, 0.0)


def shape(dims, kind=BF):
    return jax.ShapeDtypeStruct(dims, kind)


VMEM = pl.BlockSpec(memory_space=pltpu.VMEM)
SMEM = pl.BlockSpec(memory_space=pltpu.SMEM)
ANY = pl.BlockSpec(memory_space=pl.ANY)


def call(
    kernel, out_shape, in_specs, out_specs, scratch=(), flops=0, moved=0, aliases=None, grid=()
):
    return pl.pallas_call(
        kernel,
        grid=grid,
        out_shape=out_shape,
        in_specs=in_specs,
        out_specs=out_specs,
        scratch_shapes=list(scratch),
        input_output_aliases=aliases or {},
        compiler_params=pltpu.CompilerParams(vmem_limit_bytes=48 * 2**20),
        cost_estimate=pl.CostEstimate(flops=flops, bytes_accessed=moved, transcendentals=0),
    )


def low_half():
    return (iota((128, 2 * HD), 0) & 7) < 4


def fold(rows):
    first, second = rows[:, : 2 * HD], rows[:, 2 * HD :]
    low = low_half()
    even = jnp.where(low, first, pltpu.roll(second, 4, 0))
    odd = jnp.where(low, pltpu.roll(first, 124, 0), second)
    both = [part.reshape(16, 8, 2 * HD) for part in (even, odd)]
    return jnp.stack(both, axis=1).reshape(2 * 128, 2 * HD).astype(BF)


def unfold(rows):
    both = rows.astype(F32).reshape(16, 2, 8, 2 * HD)
    even = both[:, 0].reshape(128, 2 * HD)
    odd = both[:, 1].reshape(128, 2 * HD)
    low = low_half()
    first = jnp.where(low, even, pltpu.roll(odd, 4, 0))
    second = jnp.where(low, pltpu.roll(even, 124, 0), odd)
    return jnp.concatenate([first, second], axis=1).astype(BF)


def spread_out(buffer_ref, rows_ref):
    for i in range(GROUPS):
        near = slice(i * BLOCK, (i + 1) * BLOCK)
        rows_ref[i * GROUP : i * GROUP + BLOCK, :] = buffer_ref[near, : 4 * HD]
        rows_ref[i * GROUP + BLOCK : (i + 1) * GROUP, :] = unfold(buffer_ref[near, 4 * HD :])


def tail_kernel(k_ref, v_ref, tail_ref):
    half = 2 * HD
    tail_ref[:, :half] = k_ref[:, :half]
    tail_ref[:, half:] = v_ref[:, :half]


def hits(labels_ref, h):
    return ones_where(labels_ref[h] == iota((CLUSTERS, TOK), 0)).astype(BF)


def count_kernel(labels_ref, counts_ref):
    rows = []
    for h in range(2):
        total = dot(jnp.ones((8, TOK), BF), hits(labels_ref, h), NT)
        rows += [total[0:1, k * 128 : (k + 1) * 128] for k in range(4)]
    table = jnp.concatenate(rows, axis=0)
    counts_ref[...] = jnp.broadcast_to(table[None], (DEVS, 8, 128)).astype(BF)


def rank_kernel(labels_ref, within_ref):
    later = ones_where(iota((TOK, TOK), 0) < iota((TOK, TOK), 1)).astype(BF)
    within_ref[...] = jnp.zeros_like(within_ref)
    for h in range(2):
        hit = hits(labels_ref, h)
        before = dot(hit, later) * hit.astype(F32)
        within_ref[h : h + 1, :] = jnp.sum(before, axis=0, keepdims=True)


def shifts_of(attempt):
    return [(attempt * a + b) & 127 for a, b in TURNS]


def dealt(ranked, attempt):
    shifts = shifts_of(attempt)
    lane = iota((DEVS, 128), 1)
    wide = jnp.where((attempt & 1) == 0, 24, 0)
    lists = []
    for h in range(2):
        lists.append(pltpu.roll(ranked[4 * h], 64, 1) if h else ranked[4 * h])
        lists += [pltpu.roll(ranked[4 * h + k], shifts[3 * h + k - 1], 1) for k in (1, 2)]
        final = pltpu.roll(ranked[4 * h + 3], shifts[3 * h + 2], 1)
        passed = (lane >= 64 * h) & (lane < 64 * h + wide)
        lists.append(jnp.where(passed, 0.0, final))
        lists.append(pltpu.roll(jnp.where(passed, final, 0.0), GAP, 1))
    return lists


def place_kernel(
    where_ref, counts_ref, labels_ref, within_ref, q_ref, k_ref, v_ref, g_ref,
    send_ref, slot_ref, name_ref, over_ref, table, ranked, stage, sems,
):
    me = where_ref[0]
    mode = where_ref[1]
    table[...] = counts_ref[...].astype(F32).reshape(DEVS * 8, 128)
    per = [table[pl.ds(r, DEVS, stride=8), :] for r in range(8)]
    orders = []
    for h in range(2):
        key_row, key_col = [], []
        for k in range(4):
            block = per[4 * h + k]
            down = jnp.sum(block, axis=0, keepdims=True)
            across = jnp.sum(block.T, axis=1, keepdims=True)
            tie_row = (CLUSTERS - 1 - k * 128) - iota((1, 128), 1)
            tie_col = (CLUSTERS - 1 - k * 128) - iota((128, 1), 0)
            key_row.append(down * CLUSTERS + tie_row.astype(F32))
            key_col.append(across * CLUSTERS + tie_col.astype(F32))
        order = []
        for k in range(4):
            larger = jnp.zeros((128, 128), F32)
            for other in range(4):
                larger = larger + ones_where(key_col[other] > key_row[k])
            rank = jnp.sum(larger, axis=0, keepdims=True).astype(jnp.int32)
            order.append(ones_where(iota((CLUSTERS, 128), 0) == rank).astype(BF))
        amount = sum(dot(per[4 * h + k].astype(BF), order[k], NT) for k in range(4))
        for k in range(4):
            ranked[4 * h + k] = amount[:, k * 128 : (k + 1) * 128]
        orders.append(jnp.concatenate(order, axis=1))

    def unfit(state):
        attempt, most = state
        return jnp.logical_and(most > CAP, attempt < TRIES)

    def attempt_next(state):
        attempt, _ = state
        return attempt + 1, jnp.max(sum(dealt(ranked, attempt)))

    attempt, most = lax.while_loop(unfit, attempt_next, (jnp.int32(0), jnp.float32(CAP + 1)))
    attempt = attempt - 1
    over = most > CAP
    over_ref[...] = jnp.full((8, 128), jnp.where(over, 1.0, 0.0), F32)

    amounts = dealt(ranked, attempt)
    offsets = [jnp.zeros((DEVS, 128), F32)]
    for j in range(PARTS):
        offsets.append(offsets[-1] + amounts[j])
    begin = 3 * mode
    end = jnp.where(over, jnp.minimum(begin + 3, PARTS), jnp.where(mode == 0, PARTS, 0))
    start = offsets[0]
    for p in (1, 2, 3):
        start = jnp.where(mode == p, offsets[3 * p], start)
    own_row = iota((DEVS, 128), 0) == me
    own_lane = iota((DEVS, 128), 1) == me
    lane8 = iota((8, 128), 1)
    bases = []
    name = jnp.zeros((DEVS, 16), jnp.int32)
    slot_lane = iota((DEVS, 16), 1).astype(F32)
    for j in range(PARTS):
        base = jnp.sum(jnp.where(own_row, offsets[j] - start, 0.0), axis=0, keepdims=True)
        inside = jnp.logical_and(j >= begin, j < end)
        base = jnp.broadcast_to(base + jnp.where(inside, 0.0, -1e6), (8, 128))
        bases.append(base + (lane8 * 16).astype(F32))
        reach = jnp.sum(jnp.where(own_lane, offsets[j + 1] - start, 0.0), axis=1, keepdims=True)
        name = name + jnp.where(reach <= slot_lane, 1, 0)
    name_ref[...] = name

    shifts = shifts_of(attempt)
    wide = jnp.where((attempt & 1) == 0, 24, 0)
    spots = []
    slot_ref[...] = jnp.zeros_like(slot_ref)
    for h in range(2):
        mine = bases[5 * h : 5 * h + 5]
        passed = (lane8 >= 64 * h) & (lane8 < 64 * h + wide)
        final = jnp.where(passed, pltpu.roll(mine[4], 128 - GAP, 1), mine[3])
        rolled = [pltpu.roll(mine[0], 64, 1) if h else mine[0]]
        for k, base in ((1, mine[1]), (2, mine[2]), (3, final)):
            rolled.append(pltpu.roll(base, (128 - shifts[3 * h + k - 1]) & 127, 1))
        column = jnp.concatenate(
            [jnp.broadcast_to(base[0:1], (128, 128)).T[:, 0:1] for base in rolled], axis=0
        )
        hit = ones_where(labels_ref[h] == iota((CLUSTERS, TOK), 0)).astype(BF)
        at = dot(orders[h], hit)
        flat = jnp.sum(at * column, axis=0, keepdims=True) + within_ref[h : h + 1, :]
        flat = flat.astype(jnp.int32)
        owner, slot = flat >> 4, flat & 15
        inner = owner & 31
        spot = jnp.where(slot < 8, inner * 8 + slot, BLOCK + inner * 4 + slot - 8)
        spot = jnp.where(flat >= 0, (owner >> 5) * GROUP + spot, -1)
        slot_ref[h : h + 1, :] = spot
        spots.append(spot)
    packed = [
        jnp.concatenate([ref[:, (2 + h) * HD : (3 + h) * HD] for ref in (q_ref, k_ref, v_ref, g_ref)], axis=1)
        for h in range(2)
    ]
    rows = iota((GROUP, TOK), 0)
    copies = []
    for i in range(GROUPS):
        total = 0.0
        for h in range(2):
            pick = ones_where(rows + i * GROUP == spots[h]).astype(BF)
            total = total + dot(pick, packed[h])
        copies.append(store_group(total, i, stage, send_ref, sems))
    for copy in copies:
        copy.wait()


def store_group(total, i, stage, to_ref, sems):
    near = pl.ds(i * BLOCK, BLOCK)
    stage[near, : 4 * HD] = total[:BLOCK].astype(BF)
    stage[near, 4 * HD :] = fold(total[BLOCK:])
    copy = pltpu.make_async_copy(stage.at[near], to_ref.at[near], sems.at[i])
    copy.start()
    return copy


def attend(q, k, v, g, keep):
    scores = jnp.where(keep, dot(q, k, NT) * (FACTOR * math.log2(math.e)), MASKED)
    raised = jnp.exp2(scores - jnp.max(scores, axis=1, keepdims=True))
    weights = raised * (1.0 / jnp.sum(raised, axis=1, keepdims=True))
    rounded = weights.astype(BF)
    out = dot(rounded, v).astype(BF)
    row_dot = jnp.sum(g.astype(F32) * out.astype(F32), axis=1, keepdims=True)
    grad_score = (weights * (dot(g, v, NT) - row_dot)).astype(BF)
    grad_k = dot(q, grad_score, TN).T * FACTOR
    return out, dot(grad_score, k) * FACTOR, grad_k, dot(g, rounded, TN).T


def position(index):
    rest = index - BLOCK
    near = (index >> 3) * 16 + (index & 7)
    far = (rest >> 2) * 16 + 8 + (rest & 3)
    return jnp.where(index < BLOCK, near, far)


def routed_kernel(
    got_ref, name_col_ref, name_row_ref, out_ref, rows, gk_sum, gv_sum, stage, sems
):
    spread_out(got_ref, rows)
    copies = []
    for i in reversed(range(GROUPS)):
        here = slice(i * GROUP, (i + 1) * GROUP)
        upto = slice(0, (i + 1) * GROUP)
        same = name_col_ref[here, :] == name_row_ref[:, upto]
        past = position(iota((1, GROUP), 1)) <= position(iota((GROUP, 1), 0))
        if i:
            past = jnp.concatenate([jnp.full((GROUP, i * GROUP), True), past], axis=1)
        out, gq, gk, gv = attend(
            rows[here, 0:HD],
            rows[upto, HD : 2 * HD],
            rows[upto, 2 * HD : 3 * HD],
            rows[here, 3 * HD :],
            same & past,
        )
        if i == GROUPS - 1:
            gk_sum[...] = gk
            gv_sum[...] = gv
        else:
            gk_sum[upto, :] += gk
            gv_sum[upto, :] += gv
        total = jnp.concatenate([out.astype(F32), gq, gk_sum[here, :], gv_sum[here, :]], axis=1)
        copies.append(store_group(total, i, stage, out_ref, sems))
    for copy in copies:
        copy.wait()


def window_kernel(
    where_ref, q_ref, k_ref, v_ref, g_ref, halo_ref, out_ref, gq_ref, gk_ref, gv_ref, edge_ref
):
    first = where_ref[0] == 0
    row = iota((BLOCK, 2 * BLOCK), 0)
    lane = iota((BLOCK, 2 * BLOCK), 1)
    band = (lane <= row + BLOCK) & (lane >= row)
    for h in range(2):
        at = slice(h * HD, (h + 1) * HD)
        at_v = slice((2 + h) * HD, (3 + h) * HD)
        k0 = jnp.concatenate([halo_ref[:, at], k_ref[0:BLOCK, at]], axis=0)
        v0 = jnp.concatenate([halo_ref[:, at_v], v_ref[0:BLOCK, at]], axis=0)
        keep = band & (lane >= jnp.where(first, BLOCK, 0))
        out, gq, gk, gv = attend(q_ref[0:BLOCK, at], k0, v0, g_ref[0:BLOCK, at], keep)
        out_ref[0:BLOCK, at] = out
        gq_ref[0:BLOCK, at] = gq.astype(BF)
        edge_ref[:, at] = gk[0:BLOCK].astype(BF)
        edge_ref[:, at_v] = gv[0:BLOCK].astype(BF)
        out, gq, gk1, gv1 = attend(
            q_ref[BLOCK:, at], k_ref[:, at], v_ref[:, at], g_ref[BLOCK:, at], band
        )
        out_ref[BLOCK:, at] = out
        gq_ref[BLOCK:, at] = gq.astype(BF)
        gk_ref[0:BLOCK, at] = gk[BLOCK:] + gk1[0:BLOCK]
        gk_ref[BLOCK:, at] = gk1[BLOCK:]
        gv_ref[0:BLOCK, at] = gv[BLOCK:] + gv1[0:BLOCK]
        gv_ref[BLOCK:, at] = gv1[BLOCK:]


def edge_kernel(gk_l, gv_l, edge_ref, gk_ref, gv_ref):
    half = 2 * HD
    for ref, mine, edge in (
        (gk_ref, gk_l, edge_ref[:, 0:half]),
        (gv_ref, gv_l, edge_ref[:, half:]),
    ):
        ref[0 : TOK - WINDOW, 0:half] = mine[0 : TOK - WINDOW, :].astype(BF)
        ref[TOK - WINDOW :, 0:half] = (mine[TOK - WINDOW :, :] + edge.astype(F32)).astype(BF)


def fetch(slot_ref, rows_ref, h):
    spot = slot_ref[h : h + 1, :].astype(F32)
    spot = jnp.broadcast_to(spot, (128, TOK)).T[:, 0:1].astype(jnp.int16)
    lane = lax.broadcasted_iota(jnp.int16, (TOK, ROWS), 1)
    return dot(jnp.where(lane == spot, BF(1), BF(0)), rows_ref[...])


def finish_kernel(slot_ref, back_ref, *refs):
    outs = refs[4:8]
    rows, stage, sems = refs[8:]
    spread_out(back_ref, rows)
    copies = []
    for h in range(2):
        found = fetch(slot_ref, rows, h).astype(BF)
        for n in range(4):
            stage[n, h] = found[:, n * HD : (n + 1) * HD]
            copy = pltpu.make_async_copy(
                stage.at[n, h], outs[n].at[:, pl.ds((2 + h) * HD, HD)], sems.at[n, h]
            )
            copy.start()
            copies.append(copy)
    for copy in copies:
        copy.wait()


def add_kernel(slot_ref, back_ref, *refs):
    before, after, rows = refs[0:4], refs[4:8], refs[8]
    spread_out(back_ref, rows)
    for n in range(4):
        after[n][:, 0 : 2 * HD] = before[n][:, 0 : 2 * HD]
    for h in range(2):
        to = slice((2 + h) * HD, (3 + h) * HD)
        found = fetch(slot_ref, rows, h)
        for n in range(4):
            more = before[n][:, to].astype(F32) + found[:, n * HD : (n + 1) * HD]
            after[n][:, to] = more.astype(BF)


def across(rows):
    blocks = rows.reshape((DEVS, 8, WIDE))
    blocks = lax.all_to_all(blocks, "seq", split_axis=0, concat_axis=0, tiled=True)
    return blocks.reshape((NEAR, WIDE))


def local(queries, keys, values, out_grad, labels):
    half = 2 * HD
    full = shape((TOK, 4 * HD))
    me = lax.axis_index("seq").astype(jnp.int32)
    sources = (queries, keys, values, out_grad)
    labels = labels.reshape(2, 1, TOK)
    last_rows = pl.BlockSpec((WINDOW, 4 * HD), lambda i: (TOK // WINDOW - 1, 0))
    tail = call(
        tail_kernel,
        shape((WINDOW, 4 * HD)),
        [last_rows] * 2,
        pl.BlockSpec((WINDOW, 4 * HD), lambda i: (0, 0)),
        moved=2**19,
        grid=(1,),
    )(keys, values)
    steps = [(s, s + 1) for s in range(DEVS - 1)]
    halo = lax.ppermute(tail, "seq", steps)
    counts = call(
        count_kernel,
        shape((DEVS, 8, 128)),
        [VMEM],
        VMEM,
        flops=2 * 2 * 8 * TOK**2,
        moved=2**18,
    )(labels)
    counts = lax.all_to_all(counts, "seq", split_axis=0, concat_axis=0, tiled=True)
    within = call(
        rank_kernel, shape((8, TOK), F32), [VMEM], VMEM, flops=2 * 2 * TOK**3, moved=2**15
    )(labels)
    counts, halo, within = lax.optimization_barrier((counts, halo, within))

    def window(halo):
        return call(
            window_kernel,
            (
                full,
                full,
                shape((TOK, half), F32),
                shape((TOK, half), F32),
                shape((WINDOW, 2 * half)),
            ),
            [SMEM] + [VMEM] * 5,
            (VMEM,) * 5,
            flops=4 * 6 * 2 * 256 * 512 * 128,
            moved=6 * 2**20,
        )(me.reshape(1), *sources, halo)

    def serve(mode, halo=None):
        send, slot, name, over = call(
            place_kernel,
            (
                shape((NEAR, WIDE)),
                shape((8, TOK), jnp.int32),
                shape((DEVS, 16), jnp.int32),
                shape((8, 128), F32),
            ),
            [SMEM] + [VMEM] * 7,
            (ANY, VMEM, VMEM, VMEM),
            scratch=(
                pltpu.VMEM((DEVS * 8, 128), F32),
                pltpu.VMEM((8, DEVS, 128), F32),
                pltpu.VMEM((NEAR, WIDE), BF),
                pltpu.SemaphoreType.DMA((GROUPS,)),
            ),
            flops=2 * 2 * ROWS * TOK * TOK,
            moved=6 * 2**20,
        )(jnp.stack([me, mode]), counts, labels, within, *sources)
        mine = None
        if halo is not None:
            send, halo = lax.optimization_barrier((send, halo))
        got = across(send)
        if halo is not None:
            *mine, edge = window(halo)
            edge = lax.ppermute(edge, "seq", [(b, a) for a, b in steps])
            got, edge = lax.optimization_barrier((got, edge))
        near = name[:, :8].reshape(GROUPS, BLOCK)
        far = name[:, 8:CAP].reshape(GROUPS, GROUP - BLOCK)
        names = jnp.concatenate([near, far], axis=1)
        results = call(
            routed_kernel,
            shape((NEAR, WIDE)),
            [VMEM] * 3,
            ANY,
            scratch=(
                pltpu.VMEM((ROWS, 4 * HD), BF),
                pltpu.VMEM((ROWS, HD), F32),
                pltpu.VMEM((ROWS, HD), F32),
                pltpu.VMEM((NEAR, WIDE), BF),
                pltpu.SemaphoreType.DMA((GROUPS,)),
            ),
            flops=6 * ROWS * ROWS * HD,
            moved=4 * 2**20,
        )(got, names.reshape(ROWS, 1), names.reshape(1, ROWS))
        if halo is not None:
            mine.append(edge)
        return across(results), slot, over, mine

    back, slot, over, (out_l, gq_l, gk_l, gv_l, edge) = serve(jnp.int32(0), halo)
    for distance in (1, 2):
        turn = [(x, (x + distance) % 4) for x in range(4)]
        over = jnp.maximum(over, lax.ppermute(over, "head", turn))
    gk_l, gv_l = call(
        edge_kernel, (full, full), [VMEM] * 3, (VMEM,) * 2, flops=2**20, moved=2**21
    )(gk_l, gv_l, edge)
    rows_scratch = pltpu.VMEM((ROWS, 4 * HD), BF)
    results = call(
        finish_kernel,
        (full,) * 4,
        [VMEM, VMEM] + [ANY] * 4,
        (ANY,) * 4,
        scratch=(
            rows_scratch,
            pltpu.VMEM((4, 2, TOK, HD), BF),
            pltpu.SemaphoreType.DMA((4, 2)),
        ),
        flops=2 * 2 * ROWS * TOK * TOK,
        moved=6 * 2**20,
        aliases={2: 0, 3: 1, 4: 2, 5: 3},
    )(slot, back, out_l, gq_l, gk_l, gv_l)
    last = jnp.where(over[0, 0] > 0.5, 4, 1).astype(jnp.int32)

    def again(mode, sums):
        more, spot, _, _ = serve(mode)
        return call(
            add_kernel, (full,) * 4, [VMEM] * 6, (VMEM,) * 4, scratch=(rows_scratch,)
        )(spot, more, *sums)

    return lax.fori_loop(1, last, again, results)


def solution(mesh):
    spec = P("seq", "head")
    return jax.shard_map(
        local,
        mesh=mesh,
        in_specs=(spec, spec, spec, spec, P("head", "seq", None)),
        out_specs=(spec, spec, spec, spec),
        check_vma=False,
    )
```
